512 devices in a mesh: inner: 32 (over x_hi, y, core), outer: 16 (over z, x_lo).
Axes of the slice: x: 4 (x_hi: 2, x_lo: 2; x = x_hi * 2 + x_lo), y: 8, z: 8, core: 2. Of those that a mesh axis runs over, the one named last changes fastest.
Arguments:
- tokens: bfloat16 [65536, 8192], P(('inner', 'outer')), may hold values from -3600 to 3600
- cotangent: bfloat16 [65536, 256], P(('inner', 'outer')), may hold values from -10 to 10
- kv_weight: bfloat16 [8192, 256], P('inner'), may hold values from -0.0625 to 0.0625
- norm_gain: bfloat16 [8192], P('inner'), may hold values from 0.5 to 1.5
Outputs:
- kv_out: bfloat16 [65536, 256], P(('inner', 'outer'))
- token_grad: bfloat16 [65536, 8192], P(('inner', 'outer'))
- kv_grad: bfloat16 [8192, 256], P(('inner', 'outer'))
- gain_grad: bfloat16 [8192], P(('inner', 'outer'))
The draws below stay inside these ranges and needn't reach their ends.
All inputs are finite; a program needn't handle non-finite values.
Results may differ from the reference program's by a relative error of at most 0.02.
Values may be sent and summed in bfloat16 or wider, within the bound.
No kernel may reach another device: no remote copies, remote signals or barrier semaphores. Data moves between devices by JAX's collectives and lax.ppermute only.
A program may use at most 64 MiB of HBM per device.

```python
import math
import jax
import jax.numpy as jnp
from jax import lax

D = 8192
HD = 128
TOK_DEV = 128
TOKENS = 65536
N_INNER = 32
N_OUTER = 16


def draw_tokens(key, part):
    key = jax.random.fold_in(key, 7)
    subkeys = jax.random.split(key, 4)
    values = jnp.clip(jax.random.normal(subkeys[0], (TOKENS, D), jnp.float32), -4.0, 4.0)
    row_spread = 10.0
    row_scale = jnp.exp(jax.random.uniform(subkeys[1], (TOKENS, 1), jnp.float32) * jnp.log(row_spread))
    col_scale = jnp.exp(jax.random.uniform(subkeys[2], (1, D), jnp.float32) * jnp.log(10.0))
    block_count = TOKENS // TOK_DEV
    block_width = D // block_count
    owners = jax.random.permutation(subkeys[3], block_count)
    target = owners[jnp.arange(TOKENS) // TOK_DEV]
    col_block = jnp.arange(D) // block_width
    emphasis = jnp.where(target[:, None] == col_block[None, :], 6.0, 1.0)
    return (values * row_scale * col_scale * emphasis).astype(jnp.bfloat16)


def levels(key, dims, cuts, smallest, largest):
    level = 1.0
    for position, shards_of in cuts:
        steps = jax.random.uniform(jax.random.fold_in(jax.random.fold_in(key, 6), position), (shards_of,), jnp.float32, smallest / len(cuts), largest / len(cuts))
        level = level * jnp.repeat(jnp.exp(steps), dims[position] // shards_of).reshape((-1,) + (1,) * (len(dims) - 1 - position))
    return level


def noise(stream_key, shape, deviation, limit, shards=(), held_as=jnp.bfloat16):
    loudness = levels(stream_key, shape, shards, -0.22, 0.18) if shards else 1.0
    result = jax.random.normal(stream_key, shape, jnp.float32) * deviation * loudness
    return jnp.minimum(jnp.maximum(result, -limit), limit).astype(held_as)


def setup_inputs(seed: int = 0) -> dict:
    streams_of = jax.random.split(jax.random.key(seed), 5)
    tokens = draw_tokens(jax.random.fold_in(streams_of[4], 71), 0)
    cotangent = noise(streams_of[1], (TOKENS, 2 * HD), 2.0, 10.0, ((0, 512),))
    kv_weight = noise(streams_of[2], (D, 2 * HD), D ** -0.5, 0.0625, ((0, 32),))
    norm_gain = jnp.clip(1.0 + 0.1 * jax.random.normal(streams_of[3], (D,), jnp.float32), 0.5, 1.5).astype(jnp.bfloat16)
    return dict(tokens=tokens, cotangent=cotangent, kv_weight=kv_weight, norm_gain=norm_gain)


def device_terms(tok_block, cot_block, weight, gains, factor):
    wide_tokens = tok_block.astype(jnp.float32)
    inv_rms = lax.rsqrt(lax.optimization_barrier(jnp.mean(wide_tokens * wide_tokens, -1, keepdims=True)) + 1e-05)
    unit_rows = wide_tokens * inv_rms
    gain_wide = gains.astype(jnp.float32)
    normed = (unit_rows * gain_wide).astype(jnp.bfloat16)
    kv_block = jnp.dot(normed, weight, preferred_element_type=jnp.float32).astype(jnp.bfloat16)
    back_rows = lax.dot_general(cot_block, weight, (((1,), (1,)), ((), ())), preferred_element_type=jnp.float32)
    unit_grad = back_rows * gain_wide
    slopes = lax.optimization_barrier(jnp.mean(unit_grad * unit_rows, -1, keepdims=True))
    grad_block = (inv_rms * (unit_grad - unit_rows * slopes)).astype(jnp.bfloat16)
    gain_term = (lax.optimization_barrier(jnp.sum(back_rows * unit_rows, 0)) * factor).astype(jnp.bfloat16)
    weight_term = (lax.dot_general(normed, cot_block, (((0,), (0,)), ((), ())), preferred_element_type=jnp.float32) * factor).astype(jnp.bfloat16)
    return (kv_block, grad_block, weight_term, gain_term)

def reference(tokens, cotangent, kv_weight, norm_gain):
    factor = 1.0 / math.sqrt(TOKENS)
    token_groups = tokens.reshape(N_INNER, N_OUTER, TOK_DEV, D).transpose(1, 0, 2, 3)
    cot_groups = cotangent.reshape(N_INNER, N_OUTER, TOK_DEV, 2 * HD).transpose(1, 0, 2, 3)

    def group(group_items):

        def absorb(totals, device_item):
            kv_block, grad_block, weight_term, gain_term = device_terms(device_item[0], device_item[1], kv_weight, norm_gain, factor)
            return ((totals[0] + weight_term.astype(jnp.float32), totals[1] + gain_term.astype(jnp.float32)), (kv_block, grad_block))
        start_totals = (jnp.zeros((D, 2 * HD), jnp.float32), jnp.zeros((D,), jnp.float32))
        sums, blocks = lax.scan(absorb, start_totals, group_items)
        return (sums[0].astype(jnp.bfloat16), sums[1].astype(jnp.bfloat16), blocks[0], blocks[1])
    weight_parts, gain_parts, kv_blocks, grad_blocks = lax.map(group, (token_groups, cot_groups))
    kv_grad = lax.optimization_barrier(jnp.sum(weight_parts.astype(jnp.float32), 0)).astype(jnp.bfloat16)
    gain_grad = lax.optimization_barrier(jnp.sum(gain_parts.astype(jnp.float32), 0)).astype(jnp.bfloat16)
    kv_out = kv_blocks.transpose(1, 0, 2, 3).reshape(TOKENS, 2 * HD)
    token_grad = grad_blocks.transpose(1, 0, 2, 3).reshape(TOKENS, D)
    return (kv_out, token_grad, kv_grad, gain_grad)
```

```python
import functools

import jax
import jax.numpy as jnp
from jax import lax
from jax.experimental import pallas as pl
from jax.experimental.pallas import tpu as pltpu
from jax.sharding import Mesh, PartitionSpec as P

AXES = ("xh", "y", "c", "z", "xl")
F32, BF16 = jnp.float32, jnp.bfloat16


def prep_kernel(core, tokens, cot, sent, scaled, inv, total):
    step = pl.program_id(0)
    other = 1 - core[0]
    wide = tokens[...].astype(F32)
    part = jnp.sum(wide * wide, -1, keepdims=True)

    @pl.when(step == 0)
    def _():
        total[...] = part

    @pl.when(step > 0)
    def _():
        total[...] += part

    for j in range(sent.shape[1] // 256):
        start = pl.multiple_of(512 * j + 256 * other, 256)
        sent[:, 256 * j : 256 * (j + 1)] = tokens[:, pl.ds(start, 256)]

    @pl.when(step == pl.num_programs(0) - 1)
    def _():
        width = tokens.shape[1] * pl.num_programs(0)
        root = lax.rsqrt(total[...] / width + 1e-05)
        inv[...] = jnp.broadcast_to(root, inv.shape)
        scaled[...] = (cot[...].astype(F32) * root).astype(BF16)


def prep(core, tokens, cot):
    rows, width = tokens.shape
    steps = 4
    return pl.pallas_call(
        prep_kernel,
        grid_spec=pltpu.PrefetchScalarGridSpec(
            num_scalar_prefetch=1,
            grid=(steps,),
            in_specs=[
                pl.BlockSpec((rows, width // steps), lambda i, c: (0, i)),
                pl.BlockSpec(cot.shape, lambda i, c: (0, 0)),
            ],
            out_specs=[
                pl.BlockSpec((rows, width // steps // 2), lambda i, c: (0, i)),
                pl.BlockSpec(cot.shape, lambda i, c: (0, 0)),
                pl.BlockSpec((rows, 128), lambda i, c: (0, 0)),
            ],
            scratch_shapes=[pltpu.VMEM((rows, 1), F32)],
        ),
        out_shape=[
            jax.ShapeDtypeStruct((rows, width // 2), BF16),
            jax.ShapeDtypeStruct(cot.shape, BF16),
            jax.ShapeDtypeStruct((rows, 128), F32),
        ],
        compiler_params=pltpu.CompilerParams(vmem_limit_bytes=16 << 20),
        cost_estimate=pl.CostEstimate(flops=2 * rows * width, bytes_accessed=3 * rows * width, transcendentals=0),
    )(core, tokens, cot)


def outer_kernel(core, tokens, got, mine, theirs, out):
    own = core[0]
    blocks = got.shape[1] // 256
    for j in range(blocks):
        start = pl.multiple_of(512 * j + 256 * own, 256)
        left = jnp.concatenate([tokens[:, pl.ds(start, 256)], got[:, 256 * j : 256 * (j + 1)]], 0)
        right = jnp.concatenate([mine[...], theirs[...]], 0)
        u = lax.dot_general(left, right, (((0,), (0,)), ((), ())), preferred_element_type=F32)
        u = u.reshape(8, 2, 16, 256).astype(BF16)
        for xl in range(2):
            out[0, xl, j] = u[:, xl]


def outer_terms(core, tokens, got, mine, theirs):
    rows, width = tokens.shape
    steps = 4
    per = 16 // steps
    return pl.pallas_call(
        outer_kernel,
        grid_spec=pltpu.PrefetchScalarGridSpec(
            num_scalar_prefetch=1,
            grid=(steps,),
            in_specs=[
                pl.BlockSpec((rows, width // steps), lambda i, c: (0, i)),
                pl.BlockSpec((rows, width // 2 // steps), lambda i, c: (0, i)),
                pl.BlockSpec(mine.shape, lambda i, c: (0, 0)),
                pl.BlockSpec(mine.shape, lambda i, c: (0, 0)),
            ],
            out_specs=pl.BlockSpec(
                (1, 2, per, 8, 16, 256), lambda i, c: (i // 2, 0, i % 2, 0, 0, 0)
            ),
        ),
        out_shape=jax.ShapeDtypeStruct((2, 2, 8, 8, 16, 256), BF16),
        compiler_params=pltpu.CompilerParams(vmem_limit_bytes=16 << 20),
        cost_estimate=pl.CostEstimate(flops=2 * rows * width * 256, bytes_accessed=6 * rows * width, transcendentals=0),
    )(core, tokens, got, mine, theirs)


def final_kernel(core, tokens, cot, inv, w_mine, w_theirs, kv_out, token_grad):
    own = core[0]
    rows, width = tokens.shape
    total = jnp.zeros((rows, 256), F32)
    pieces = []
    for xh in range(2):
        for y in range(8):
            for ref, side in ((w_mine, own), (w_theirs, 1 - own)):
                start = pl.multiple_of(512 * (8 * xh + y) + 256 * side, 256)
                pieces.append((ref, xh, y, start))
    for ref, xh, y, start in pieces:
        w = jnp.concatenate([ref[xh, 0, y], ref[xh, 1, y]], 0)
        total += jnp.dot(tokens[:, pl.ds(start, 256)], w, preferred_element_type=F32)
    root = inv[:, :1]
    kv = total * root
    kv_out[...] = kv.astype(BF16)
    slopes = jnp.sum(cot[...].astype(F32) * kv, -1, keepdims=True) * (1.0 / width)
    slopes = root * slopes
    for ref, xh, y, start in pieces:
        w = jnp.concatenate([ref[xh, 0, y], ref[xh, 1, y]], 0)
        back = lax.dot_general(cot[...], w, (((1,), (1,)), ((), ())), preferred_element_type=F32)
        x = tokens[:, pl.ds(start, 256)].astype(F32)
        token_grad[:, pl.ds(start, 256)] = (root * (back - x * slopes)).astype(BF16)


def final(core, tokens, cot, inv, w_mine, w_theirs):
    vmem = pl.BlockSpec(memory_space=pltpu.VMEM)
    return pl.pallas_call(
        final_kernel,
        in_specs=[pl.BlockSpec(memory_space=pltpu.SMEM)] + [vmem] * 5,
        out_specs=[vmem, vmem],
        out_shape=[
            jax.ShapeDtypeStruct(cot.shape, BF16),
            jax.ShapeDtypeStruct(tokens.shape, BF16),
        ],
        compiler_params=pltpu.CompilerParams(vmem_limit_bytes=24 << 20),
        cost_estimate=pl.CostEstimate(flops=4 * tokens.size * 256, bytes_accessed=8 << 20, transcendentals=0),
    )(core, tokens, cot, inv, w_mine, w_theirs)


SWAP = [(0, 1), (1, 0)]


def body(tokens, cotangent, kv_weight, norm_gain):
    factor = 1.0 / 256.0
    core = lax.axis_index("c").astype(jnp.int32).reshape(1)
    half = lax.axis_index("xl")
    piece = 2 * lax.axis_index("z") + half
    gain = norm_gain.astype(F32)[:, None]
    wide = kv_weight.astype(F32)
    scaled_weight = (wide * gain).astype(BF16)

    share = lax.dynamic_slice_in_dim(scaled_weight, 128 * half, 128, 0)
    along_y = lax.all_to_all(jnp.broadcast_to(share, (8, 128, 256)), "y", 0, 0, tiled=True)
    w_mine = lax.all_to_all(
        jnp.broadcast_to(along_y, (4, 8, 128, 256)), ("xh", "xl"), 0, 0, tiled=True
    ).reshape(2, 2, 8, 128, 256)
    w_theirs = lax.ppermute(w_mine, "c", SWAP)

    sent, scaled, inv = prep(core, tokens, cotangent)
    got = lax.ppermute(sent, "c", SWAP)
    got_scaled = lax.ppermute(scaled, "c", SWAP)
    u = outer_terms(core, tokens, got, scaled, got_scaled)
    u = lax.all_to_all(u.reshape(4, 64, 16, 256), ("xh", "xl"), 0, 0, tiled=True)
    u = jnp.sum(u, 0, dtype=F32).astype(BF16)
    u = lax.all_to_all(u, ("y", "z"), 0, 0, tiled=True)
    u = jnp.sum(u, 0, dtype=F32) * factor
    kv_grad = (u * lax.dynamic_slice_in_dim(gain, 16 * piece, 16, 0)).astype(BF16)
    gain_grad = jnp.sum(u * lax.dynamic_slice_in_dim(wide, 16 * piece, 16, 0), -1).astype(BF16)

    kv_out, token_grad = final(core, tokens, cotangent, inv, w_mine, w_theirs)
    return (kv_out, token_grad, kv_grad, gain_grad)


def solution(mesh):
    split = Mesh(mesh.devices.reshape(2, 8, 2, 8, 2), AXES)
    every, inner = P(AXES, None), ("xh", "y", "c")
    return jax.shard_map(
        body,
        mesh=split,
        in_specs=(every, every, P(inner, None), P(inner)),
        out_specs=(every, every, every, P(AXES)),
        check_vma=False,
    )
```

```python
import jax
import jax.numpy as jnp
from jax import lax
from jax.experimental import pallas as pl
from jax.experimental.pallas import tpu as pltpu
from jax.sharding import Mesh, PartitionSpec as P

AXES = ("xh", "y", "c", "z", "xl")
F32, BF16 = jnp.float32, jnp.bfloat16


def prep_kernel(core, tokens, cot, sent, scaled, inv, total):
    step = pl.program_id(0)
    other = 1 - core[0]
    wide = tokens[...].astype(F32)
    part = jnp.sum(wide * wide, -1, keepdims=True)

    @pl.when(step == 0)
    def _():
        total[...] = part

    @pl.when(step > 0)
    def _():
        total[...] += part

    for j in range(sent.shape[1] // 256):
        start = pl.multiple_of(512 * j + 256 * other, 256)
        sent[:, 256 * j : 256 * (j + 1)] = tokens[:, pl.ds(start, 256)]

    @pl.when(step == pl.num_programs(0) - 1)
    def _():
        width = tokens.shape[1] * pl.num_programs(0)
        root = lax.rsqrt(total[...] / width + 1e-05)
        inv[...] = jnp.broadcast_to(root, inv.shape)
        scaled[...] = (cot[...].astype(F32) * root).astype(BF16)


def prep(core, tokens, cot):
    rows, width = tokens.shape
    steps = 4
    return pl.pallas_call(
        prep_kernel,
        grid_spec=pltpu.PrefetchScalarGridSpec(
            num_scalar_prefetch=1,
            grid=(steps,),
            in_specs=[
                pl.BlockSpec((rows, width // steps), lambda i, c: (0, i)),
                pl.BlockSpec(cot.shape, lambda i, c: (0, 0)),
            ],
            out_specs=[
                pl.BlockSpec((rows, width // steps // 2), lambda i, c: (0, i)),
                pl.BlockSpec(cot.shape, lambda i, c: (0, 0)),
                pl.BlockSpec((rows, 128), lambda i, c: (0, 0)),
            ],
            scratch_shapes=[pltpu.VMEM((rows, 1), F32)],
        ),
        out_shape=[
            jax.ShapeDtypeStruct((rows, width // 2), BF16),
            jax.ShapeDtypeStruct(cot.shape, BF16),
            jax.ShapeDtypeStruct((rows, 128), F32),
        ],
        compiler_params=pltpu.CompilerParams(vmem_limit_bytes=16 << 20),
        cost_estimate=pl.CostEstimate(flops=2 * rows * width, bytes_accessed=3 * rows * width, transcendentals=0),
    )(core, tokens, cot)


def outer_kernel(place, tokens, got, mine, theirs, out0, out1, out2, out3):
    core, xh, xl = place[0], place[1], place[2]
    right = jnp.concatenate([mine[...], theirs[...]], 0)
    for hi in range(2):
        outs = ((out0, out1), (out2, out3))[hi]
        for y in range(8):
            block = 8 * (hi + xh - 2 * hi * xh) + y
            start = pl.multiple_of(512 * block + 256 * core, 256)
            start_got = pl.multiple_of(256 * block, 256)
            left = jnp.concatenate([tokens[:, pl.ds(start, 256)], got[:, pl.ds(start_got, 256)]], 0)
            u = lax.dot_general(left, right, (((0,), (0,)), ((), ())), preferred_element_type=F32)
            u = u.reshape(8, 2, 16, 256)
            outs[0][y] = jnp.where(xl == 0, u[:, 0], u[:, 1]).astype(BF16)
            outs[1][y] = jnp.where(xl == 0, u[:, 1], u[:, 0]).astype(BF16)


def outer_terms(place, tokens, got, mine, theirs):
    vmem = pl.BlockSpec(memory_space=pltpu.VMEM)
    return pl.pallas_call(
        outer_kernel,
        in_specs=[pl.BlockSpec(memory_space=pltpu.SMEM)] + [vmem] * 4,
        out_specs=[vmem] * 4,
        out_shape=[jax.ShapeDtypeStruct((8, 8, 16, 256), BF16)] * 4,
        compiler_params=pltpu.CompilerParams(vmem_limit_bytes=16 << 20),
        cost_estimate=pl.CostEstimate(flops=2 * tokens.size * 256, bytes_accessed=6 * tokens.size, transcendentals=0),
    )(place, tokens, got, mine, theirs)


def final_kernel(place, tokens, cot, inv, *refs):
    core, xh, xl = place[0], place[1], place[2]
    own, other, (kv_out, token_grad) = refs[:4], refs[4:8], refs[8:]
    rows, width = tokens.shape
    g = cot[...]
    g = jnp.where(xl == 0, g, jnp.concatenate([g[:, 128:], g[:, :128]], 1))
    pieces = []
    for hi in range(2):
        for y in range(8):
            for refs_of, side in ((own, core), (other, 1 - core)):
                start = pl.multiple_of(512 * (8 * (hi + xh - 2 * hi * xh) + y) + 256 * side, 256)
                pieces.append((refs_of[2 * hi], refs_of[2 * hi + 1], y, start))
    total = jnp.zeros((rows, 256), F32)
    for a, b, y, start in pieces:
        w = jnp.concatenate([a[y], b[y]], 1)
        total += jnp.dot(tokens[:, pl.ds(start, 256)], w, preferred_element_type=F32)
    root = inv[:, :1]
    kv = total * root
    kv_out[...] = jnp.where(xl == 0, kv, jnp.concatenate([kv[:, 128:], kv[:, :128]], 1)).astype(BF16)
    slopes = jnp.sum(g.astype(F32) * kv, -1, keepdims=True) * (1.0 / width)
    slopes = root * slopes
    for a, b, y, start in pieces:
        w = jnp.concatenate([a[y], b[y]], 1)
        back = lax.dot_general(g, w, (((1,), (1,)), ((), ())), preferred_element_type=F32)
        x = tokens[:, pl.ds(start, 256)].astype(F32)
        token_grad[:, pl.ds(start, 256)] = (root * (back - x * slopes)).astype(BF16)


def final(place, tokens, cot, inv, own, other):
    vmem = pl.BlockSpec(memory_space=pltpu.VMEM)
    return pl.pallas_call(
        final_kernel,
        in_specs=[pl.BlockSpec(memory_space=pltpu.SMEM)] + [vmem] * 11,
        out_specs=[vmem, vmem],
        out_shape=[
            jax.ShapeDtypeStruct(cot.shape, BF16),
            jax.ShapeDtypeStruct(tokens.shape, BF16),
        ],
        compiler_params=pltpu.CompilerParams(vmem_limit_bytes=24 << 20),
        cost_estimate=pl.CostEstimate(flops=4 * tokens.size * 256, bytes_accessed=8 << 20, transcendentals=0),
    )(place, tokens, cot, inv, *own, *other)


SWAP = [(0, 1), (1, 0)]


def along_x(values):
    moved = {}
    for k in (2, 1, 3):
        moved[k] = lax.ppermute(values[k - 1], ("xh", "xl"), [(i, i ^ k) for i in range(4)])
    return [moved[1], moved[2], moved[3]]


def body(tokens, cotangent, kv_weight, norm_gain):
    factor = 1.0 / 256.0
    half = lax.axis_index("xl")
    place = jnp.stack([lax.axis_index("c"), lax.axis_index("xh"), half]).astype(jnp.int32)
    piece = 2 * lax.axis_index("z") + half
    gain = norm_gain.astype(F32)[:, None]
    wide = kv_weight.astype(F32)
    share = (jnp.where(half == 0, wide[:, :128], wide[:, 128:]) * gain).astype(BF16)

    sent, scaled, inv = prep(place, tokens, cotangent)
    share, inv = lax.optimization_barrier((share, inv))
    got = lax.ppermute(sent, "c", SWAP)
    got_scaled = lax.ppermute(scaled, "c", SWAP)
    terms = outer_terms(place, tokens, got, scaled, got_scaled)
    moved = along_x(terms[1:])

    along_y = lax.all_to_all(jnp.broadcast_to(share, (8, 256, 128)), "y", 0, 0, tiled=True)
    own = [along_y] + along_x([along_y] * 3)
    other = [lax.ppermute(w, "c", SWAP) for w in own]

    u = sum(m.astype(F32) for m in (terms[0], *moved)).astype(BF16)
    u = lax.all_to_all(u, "y", 0, 0, tiled=True)
    u = jnp.sum(u, 0, dtype=F32).astype(BF16)
    u = lax.all_to_all(u, "z", 0, 0, tiled=True)
    u = jnp.sum(u, 0, dtype=F32) * factor
    kv_grad = (u * lax.dynamic_slice_in_dim(gain, 16 * piece, 16, 0)).astype(BF16)
    gain_grad = jnp.sum(u * lax.dynamic_slice_in_dim(wide, 16 * piece, 16, 0), -1).astype(BF16)

    kv_out, token_grad = final(place, tokens, cotangent, inv, own, other)
    return (kv_out, token_grad, kv_grad, gain_grad)


def solution(mesh):
    split = Mesh(mesh.devices.reshape(2, 8, 2, 8, 2), AXES)
    every, inner = P(AXES, None), ("xh", "y", "c")
    return jax.shard_map(
        body,
        mesh=split,
        in_specs=(every, every, P(inner, None), P(inner)),
        out_specs=(every, every, every, P(AXES)),
        check_vma=False,
    )
```

```python
import jax
import jax.numpy as jnp
from jax import lax
from jax.experimental import pallas as pl
from jax.experimental.pallas import tpu as pltpu
from jax.sharding import Mesh, PartitionSpec as P

AXES = ("xh", "y", "c", "z", "xl")
F32, BF16 = jnp.float32, jnp.bfloat16


def prep_kernel(tokens, cot, scaled, inv):
    wide = tokens[...].astype(F32)
    root = lax.rsqrt(jnp.mean(wide * wide, -1, keepdims=True) + 1e-05)
    inv[...] = jnp.broadcast_to(root, inv.shape)
    scaled[...] = (cot[...].astype(F32) * root).astype(BF16)


def prep(tokens, cot):
    rows, width = tokens.shape
    steps = 4
    return pl.pallas_call(
        prep_kernel,
        grid=(steps,),
        in_specs=[
            pl.BlockSpec((rows // steps, width), lambda i: (i, 0)),
            pl.BlockSpec((rows // steps, 256), lambda i: (i, 0)),
        ],
        out_specs=[
            pl.BlockSpec((rows // steps, 256), lambda i: (i, 0)),
            pl.BlockSpec((rows // steps, 128), lambda i: (i, 0)),
        ],
        out_shape=[
            jax.ShapeDtypeStruct(cot.shape, BF16),
            jax.ShapeDtypeStruct((rows, 128), F32),
        ],
        compiler_params=pltpu.CompilerParams(vmem_limit_bytes=8 << 20),
        cost_estimate=pl.CostEstimate(flops=2 * rows * width, bytes_accessed=2 * rows * width, transcendentals=0),
    )(tokens, cot)


def outer_kernel(place, tokens, got, mine, theirs, out0, out1, out2, out3):
    core, xh, xl = place[0], place[1], place[2]
    right = jnp.concatenate([mine[...], theirs[...]], 0)
    for hi in range(2):
        outs = ((out0, out1), (out2, out3))[hi]
        for y in range(8):
            block = 8 * (hi + xh - 2 * hi * xh) + y
            start = pl.multiple_of(512 * block + 256 * core, 256)
            left = jnp.concatenate([tokens[:, pl.ds(start, 256)], got[:, pl.ds(start, 256)]], 0)
            u = lax.dot_general(left, right, (((0,), (0,)), ((), ())), preferred_element_type=F32)
            u = u.reshape(8, 2, 16, 256)
            outs[0][y] = jnp.where(xl == 0, u[:, 0], u[:, 1]).astype(BF16)
            outs[1][y] = jnp.where(xl == 0, u[:, 1], u[:, 0]).astype(BF16)


def outer_terms(place, tokens, got, mine, theirs):
    vmem = pl.BlockSpec(memory_space=pltpu.VMEM)
    return pl.pallas_call(
        outer_kernel,
        in_specs=[pl.BlockSpec(memory_space=pltpu.SMEM)] + [vmem] * 4,
        out_specs=[vmem] * 4,
        out_shape=[jax.ShapeDtypeStruct((8, 8, 16, 256), BF16)] * 4,
        compiler_params=pltpu.CompilerParams(vmem_limit_bytes=10 << 20),
        cost_estimate=pl.CostEstimate(flops=2 * tokens.size * 256, bytes_accessed=6 * tokens.size, transcendentals=0),
    )(place, tokens, got, mine, theirs)


def final_kernel(place, tokens, cot, inv, own_a, own_b, other_a, other_b, kv_out, token_grad):
    core, xh, parity = place[0], place[1], place[3]
    rows, width = tokens.shape
    g = cot[...]
    g = jnp.where(parity == 0, g, jnp.concatenate([g[:, 128:], g[:, :128]], 1))
    pieces = []
    for hi in range(2):
        for y in range(8):
            for a, b, side in ((own_a, own_b, core), (other_a, other_b, 1 - core)):
                start = pl.multiple_of(512 * (8 * (hi + xh - 2 * hi * xh) + y) + 256 * side, 256)
                pieces.append((a, b, y, hi, start))
    total = jnp.zeros((rows, 256), F32)
    for a, b, y, hi, start in pieces:
        w = jnp.concatenate([a[y, hi], b[y, hi]], 1)
        total += jnp.dot(tokens[:, pl.ds(start, 256)], w, preferred_element_type=F32)
    root = inv[:, :1]
    kv = total * root
    kv_out[...] = jnp.where(parity == 0, kv, jnp.concatenate([kv[:, 128:], kv[:, :128]], 1)).astype(BF16)
    slopes = jnp.sum(g.astype(F32) * kv, -1, keepdims=True) * (1.0 / width)
    slopes = root * slopes
    for a, b, y, hi, start in pieces:
        w = jnp.concatenate([a[y, hi], b[y, hi]], 1)
        back = lax.dot_general(g, w, (((1,), (1,)), ((), ())), preferred_element_type=F32)
        x = tokens[:, pl.ds(start, 256)].astype(F32)
        token_grad[:, pl.ds(start, 256)] = (root * (back - x * slopes)).astype(BF16)


def final(place, tokens, cot, inv, weights):
    vmem = pl.BlockSpec(memory_space=pltpu.VMEM)
    return pl.pallas_call(
        final_kernel,
        in_specs=[pl.BlockSpec(memory_space=pltpu.SMEM)] + [vmem] * 7,
        out_specs=[vmem, vmem],
        out_shape=[
            jax.ShapeDtypeStruct(cot.shape, BF16),
            jax.ShapeDtypeStruct(tokens.shape, BF16),
        ],
        compiler_params=pltpu.CompilerParams(vmem_limit_bytes=14 << 20),
        cost_estimate=pl.CostEstimate(flops=4 * tokens.size * 256, bytes_accessed=8 << 20, transcendentals=0),
    )(place, tokens, cot, inv, *weights)


SWAP = [(0, 1), (1, 0)]


def along_x(values):
    moved = {}
    for k in (2, 1, 3):
        moved[k] = lax.ppermute(values[k - 1], ("xh", "xl"), [(i, i ^ k) for i in range(4)])
    return [moved[1], moved[2], moved[3]]


ALONG_Z = [(z, z ^ 1) for z in range(8)] + [(8 + z, 8 + (z + 1 if z % 2 else z - 1) % 8) for z in range(8)]


def body(tokens, cotangent, kv_weight, norm_gain):
    factor = 1.0 / 256.0
    half = lax.axis_index("xl")
    along_z = lax.axis_index("z")
    parity = along_z % 2
    place = jnp.stack([lax.axis_index("c"), lax.axis_index("xh"), half, parity]).astype(jnp.int32)
    piece = 2 * along_z + half
    gain = norm_gain.astype(F32)[:, None]

    scaled_weight = (kv_weight.astype(F32) * gain).astype(BF16)
    across = lax.ppermute(scaled_weight, ("xh", "xl"), [(i, i ^ 3) for i in range(4)])

    got = lax.ppermute(tokens, "c", SWAP)
    scaled, inv = prep(tokens, cotangent)
    got_scaled = lax.ppermute(scaled, "c", SWAP)
    share = jnp.stack([scaled_weight, across])
    share = jnp.where(parity == 0, share[:, :, :128], share[:, :, 128:])
    share, got_scaled = lax.optimization_barrier((share, got_scaled))
    own_a = lax.all_to_all(jnp.broadcast_to(share, (8, 2, 256, 128)), "y", 0, 0, tiled=True)
    own_b = lax.ppermute(own_a, ("c", "z"), ALONG_Z)
    other_a = lax.ppermute(own_a, "c", SWAP)
    other_b = lax.ppermute(own_b, "c", SWAP)

    terms = outer_terms(place, tokens, got, scaled, got_scaled)
    moved = along_x(terms[1:])
    u = sum(m.astype(F32) for m in (terms[0], *moved)).astype(BF16)
    u = lax.all_to_all(u, "y", 0, 0, tiled=True)
    u = jnp.sum(u, 0, dtype=F32).astype(BF16)
    u = lax.all_to_all(u, "z", 0, 0, tiled=True)
    u = jnp.sum(u, 0, dtype=F32) * factor
    kv_grad = (u * lax.dynamic_slice_in_dim(gain, 16 * piece, 16, 0)).astype(BF16)
    rows = lax.dynamic_slice_in_dim(kv_weight, 16 * piece, 16, 0).astype(F32)
    gain_grad = jnp.sum(u * rows, -1).astype(BF16)

    kv_out, token_grad = final(place, tokens, cotangent, inv, (own_a, own_b, other_a, other_b))
    return (kv_out, token_grad, kv_grad, gain_grad)


def solution(mesh):
    split = Mesh(mesh.devices.reshape(2, 8, 2, 8, 2), AXES)
    every, inner = P(AXES, None), ("xh", "y", "c")
    return jax.shard_map(
        body,
        mesh=split,
        in_specs=(every, every, P(inner, None), P(inner)),
        out_specs=(every, every, every, P(AXES)),
        check_vma=False,
    )
```

```python
import itertools
import math

import jax
import jax.numpy as jnp
import numpy as np
from jax import lax
from jax.experimental import pallas as pl
from jax.experimental.pallas import tpu as pltpu
from jax.sharding import Mesh, PartitionSpec as P

AXES = ("xh", "yh", "yl", "c", "zh", "zl", "xl")
SIZES = (2, 4, 2, 2, 4, 2, 2)
F32, BF16 = jnp.float32, jnp.bfloat16


def prep_kernel(tokens, cot, scaled, inv):
    wide = tokens[...].astype(F32)
    root = lax.rsqrt(jnp.mean(wide * wide, -1, keepdims=True) + 1e-05)
    inv[...] = jnp.broadcast_to(root, inv.shape)
    scaled[...] = (cot[...].astype(F32) * root).astype(BF16)


def prep(tokens, cot):
    rows, width = tokens.shape
    steps = 4
    return pl.pallas_call(
        prep_kernel,
        grid=(steps,),
        in_specs=[
            pl.BlockSpec((rows // steps, width), lambda i: (i, 0)),
            pl.BlockSpec((rows // steps, 256), lambda i: (i, 0)),
        ],
        out_specs=[
            pl.BlockSpec((rows // steps, 256), lambda i: (i, 0)),
            pl.BlockSpec((rows // steps, 128), lambda i: (i, 0)),
        ],
        out_shape=[
            jax.ShapeDtypeStruct(cot.shape, BF16),
            jax.ShapeDtypeStruct((rows, 128), F32),
        ],
        compiler_params=pltpu.CompilerParams(vmem_limit_bytes=8 << 20),
        cost_estimate=pl.CostEstimate(flops=2 * rows * width, bytes_accessed=2 * rows * width, transcendentals=0),
    )(tokens, cot)


def merge_kernel(core, tokens, got, mine, theirs, weights, out):
    right = jnp.concatenate([mine[...], theirs[...]], 0)
    for xh in range(2):
        for yh in range(4):
            for yl in range(2):
                block = 8 * xh + 2 * yh + yl
                start = pl.multiple_of(512 * block + 256 * core[0], 256)
                left = jnp.concatenate([tokens[:, pl.ds(start, 256)], got[:, pl.ds(start, 256)]], 0)
                u = lax.dot_general(left, right, (((0,), (0,)), ((), ())), preferred_element_type=F32)
                u = u.reshape(4, 2, 2, 16, 256).astype(BF16)
                first = 64 * (4 * xh + yh)
                for xl in range(2):
                    for zl in range(2):
                        out[4 * xl + 2 * yl + zl, first : first + 64] = u[:, zl, xl].reshape(64, 256)
    for k in range(8):
        out[k, 512:] = weights[...]


def merge(core, tokens, got, mine, theirs, weights):
    vmem = pl.BlockSpec(memory_space=pltpu.VMEM)
    return pl.pallas_call(
        merge_kernel,
        in_specs=[pl.BlockSpec(memory_space=pltpu.SMEM)] + [vmem] * 5,
        out_specs=vmem,
        out_shape=jax.ShapeDtypeStruct((8, 1024, 256), BF16),
        compiler_params=pltpu.CompilerParams(vmem_limit_bytes=12 << 20),
        cost_estimate=pl.CostEstimate(flops=2 * tokens.size * 256, bytes_accessed=8 * tokens.size, transcendentals=0),
    )(core, tokens, got, mine, theirs, weights)


def final_kernel(core, tokens, cot, inv, w_mine, w_theirs, kv_out, token_grad):
    rows, width = tokens.shape
    pieces = []
    for block in range(16):
        for ref, side in ((w_mine, core[0]), (w_theirs, 1 - core[0])):
            pieces.append((ref, 32 * block, pl.multiple_of(512 * block + 256 * side, 256)))
    total = jnp.zeros((rows, 256), F32)
    for ref, row, start in pieces:
        w = ref[:, row : row + 32].reshape(256, 256)
        total += jnp.dot(tokens[:, pl.ds(start, 256)], w, preferred_element_type=F32)
    root = inv[:, :1]
    kv = total * root
    kv_out[...] = kv.astype(BF16)
    g = cot[...]
    slopes = jnp.sum(g.astype(F32) * kv, -1, keepdims=True) * (1.0 / width)
    slopes = root * slopes
    for ref, row, start in pieces:
        w = ref[:, row : row + 32].reshape(256, 256)
        back = lax.dot_general(g, w, (((1,), (1,)), ((), ())), preferred_element_type=F32)
        x = tokens[:, pl.ds(start, 256)].astype(F32)
        token_grad[:, pl.ds(start, 256)] = (root * (back - x * slopes)).astype(BF16)


def final(core, tokens, cot, inv, w_mine, w_theirs):
    vmem = pl.BlockSpec(memory_space=pltpu.VMEM)
    return pl.pallas_call(
        final_kernel,
        in_specs=[pl.BlockSpec(memory_space=pltpu.SMEM)] + [vmem] * 5,
        out_specs=[vmem, vmem],
        out_shape=[
            jax.ShapeDtypeStruct(cot.shape, BF16),
            jax.ShapeDtypeStruct(tokens.shape, BF16),
        ],
        compiler_params=pltpu.CompilerParams(vmem_limit_bytes=14 << 20),
        cost_estimate=pl.CostEstimate(flops=4 * tokens.size * 256, bytes_accessed=8 << 20, transcendentals=0),
    )(core, tokens, cot, inv, w_mine, w_theirs)


SWAP = [(0, 1), (1, 0)]


def cubes():
    index = np.arange(math.prod(SIZES)).reshape(SIZES)
    groups = []
    for core in range(2):
        for x0, y0, z0 in itertools.product(range(core, 4, 2), range(core, 8, 2), range(core, 8, 2)):
            members = {}
            for a, b, c in itertools.product(range(2), repeat=3):
                x, y, z = (x0 + a) % 4, (y0 + b) % 8, (z0 + c) % 8
                members[x % 2, y % 2, z % 2] = int(index[x // 2, y // 2, y % 2, core, z // 2, z % 2, x % 2])
            groups.append([members[k] for k in sorted(members)])
    return groups


def body(tokens, cotangent, kv_weight, norm_gain):
    factor = 1.0 / 256.0
    core = lax.axis_index("c").astype(jnp.int32).reshape(1)
    xl, zl = lax.axis_index("xl"), lax.axis_index("zl")
    piece = 4 * lax.axis_index("zh") + 2 * zl + xl

    got = lax.ppermute(tokens, "c", SWAP)
    scaled, inv = prep(tokens, cotangent)
    got_scaled = lax.ppermute(scaled, "c", SWAP)

    scaled_weight = (kv_weight.astype(F32) * norm_gain.astype(F32)[:, None]).astype(BF16).reshape(2, 2, 2, 32, 256)
    share = lax.dynamic_slice(scaled_weight, (xl, 0, zl, 0, 0), (1, 2, 1, 32, 256)).reshape(2, 32, 256)
    share = jnp.broadcast_to(share, (8, 2, 32, 256)).reshape(16, 32, 256)
    share = lax.all_to_all(share, ("xh", "yh", "yl"), 0, 0, tiled=True).reshape(512, 256)

    both = merge(core, tokens, got, scaled, got_scaled, share)
    both = lax.all_to_all(both, AXES, 0, 0, tiled=True, axis_index_groups=cubes())
    u = jnp.sum(both[:, :512], 0, dtype=F32).astype(BF16).reshape(32, 16, 256)
    w_mine = both[:, 512:]
    w_theirs = lax.ppermute(w_mine, "c", SWAP)

    u = lax.all_to_all(u, ("xh", "yh", "zh"), 0, 0, tiled=True)
    kv_out, token_grad = final(core, tokens, cotangent, inv, w_mine, w_theirs)
    u, kv_out = lax.optimization_barrier((u, kv_out))
    u = jnp.sum(u, 0, dtype=F32) * factor
    gain = lax.dynamic_slice_in_dim(norm_gain, 16 * piece, 16, 0).astype(F32)
    kv_grad = (u * gain[:, None]).astype(BF16)
    rows = lax.dynamic_slice_in_dim(kv_weight, 16 * piece, 16, 0).astype(F32)
    gain_grad = jnp.sum(u * rows, -1).astype(BF16)

    return (kv_out, token_grad, kv_grad, gain_grad)


def solution(mesh):
    split = Mesh(mesh.devices.reshape(SIZES), AXES)
    every, inner = P(AXES, None), ("xh", "yh", "yl", "c")
    return jax.shard_map(
        body,
        mesh=split,
        in_specs=(every, every, P(inner, None), P(inner)),
        out_specs=(every, every, every, P(AXES)),
        check_vma=False,
    )
```

```python
import itertools
import math

import jax
import jax.numpy as jnp
import numpy as np
from jax import lax
from jax.experimental import pallas as pl
from jax.experimental.pallas import tpu as pltpu
from jax.sharding import Mesh, PartitionSpec as P

AXES = ("xh", "yh", "yl", "c", "zh", "zl", "xl")
SIZES = (2, 4, 2, 2, 4, 2, 2)
F32, BF16 = jnp.float32, jnp.bfloat16


def prep_kernel(tokens, cot, scaled, inv):
    wide = tokens[...].astype(F32)
    root = lax.rsqrt(jnp.mean(wide * wide, -1, keepdims=True) + 1e-05)
    inv[...] = jnp.broadcast_to(root, inv.shape)
    scaled[...] = (cot[...].astype(F32) * root).astype(BF16)


def prep(tokens, cot):
    rows, width = tokens.shape
    steps = 4
    return pl.pallas_call(
        prep_kernel,
        grid=(steps,),
        in_specs=[
            pl.BlockSpec((rows // steps, width), lambda i: (i, 0)),
            pl.BlockSpec((rows // steps, 256), lambda i: (i, 0)),
        ],
        out_specs=[
            pl.BlockSpec((rows // steps, 256), lambda i: (i, 0)),
            pl.BlockSpec((rows // steps, 128), lambda i: (i, 0)),
        ],
        out_shape=[
            jax.ShapeDtypeStruct(cot.shape, BF16),
            jax.ShapeDtypeStruct((rows, 128), F32),
        ],
        compiler_params=pltpu.CompilerParams(vmem_limit_bytes=8 << 20),
        cost_estimate=pl.CostEstimate(flops=2 * rows * width, bytes_accessed=2 * rows * width, transcendentals=0),
    )(tokens, cot)


def share_kernel(place, weight, gain, out, scaled):
    xl, zl = place[1], place[2]
    row = lax.broadcasted_iota(jnp.int32, (256, 256), 0)
    column = lax.broadcasted_iota(jnp.int32, (256, 256), 1)
    diagonal = jnp.where(row == column, gain[...].astype(F32), 0.0).astype(BF16)
    scaled[...] = jnp.dot(diagonal, weight[...], preferred_element_type=F32).astype(BF16)
    for yl in range(2):
        rows = scaled[pl.ds(pl.multiple_of(128 * xl + 64 * yl + 32 * zl, 32), 32), :]
        for k in range(8):
            out[2 * k + yl] = rows


def make_share(place, weight, gain):
    vmem = pl.BlockSpec(memory_space=pltpu.VMEM)
    return pl.pallas_call(
        share_kernel,
        in_specs=[pl.BlockSpec(memory_space=pltpu.SMEM), vmem, vmem],
        out_specs=vmem,
        out_shape=jax.ShapeDtypeStruct((16, 32, 256), BF16),
        scratch_shapes=[pltpu.VMEM((256, 256), BF16)],
        compiler_params=pltpu.CompilerParams(vmem_limit_bytes=4 << 20),
        cost_estimate=pl.CostEstimate(flops=1 << 25, bytes_accessed=1 << 19, transcendentals=0),
    )(place, weight, gain)


def merge_kernel(place, tokens, got, mine, theirs, weights, out):
    right = jnp.concatenate([mine[...], theirs[...]], 0)
    for xh in range(2):
        for yh in range(4):
            for yl in range(2):
                block = 8 * xh + 2 * yh + yl
                start = pl.multiple_of(512 * block + 256 * place[0], 256)
                left = jnp.concatenate([tokens[:, pl.ds(start, 256)], got[:, pl.ds(start, 256)]], 0)
                u = lax.dot_general(left, right, (((0,), (0,)), ((), ())), preferred_element_type=F32)
                u = u.reshape(4, 2, 2, 16, 256).astype(BF16)
                first = 64 * (4 * xh + yh)
                for xl in range(2):
                    for zl in range(2):
                        out[4 * xl + 2 * yl + zl, first : first + 64] = u[:, zl, xl].reshape(64, 256)
    for k in range(8):
        first = 256 * (k // 4)
        out[k, 512:] = weights[first : first + 256]


def merge(place, tokens, got, mine, theirs, weights):
    vmem = pl.BlockSpec(memory_space=pltpu.VMEM)
    return pl.pallas_call(
        merge_kernel,
        in_specs=[pl.BlockSpec(memory_space=pltpu.SMEM)] + [vmem] * 5,
        out_specs=vmem,
        out_shape=jax.ShapeDtypeStruct((8, 768, 256), BF16),
        compiler_params=pltpu.CompilerParams(vmem_limit_bytes=12 << 20),
        cost_estimate=pl.CostEstimate(flops=2 * tokens.size * 256, bytes_accessed=8 * tokens.size, transcendentals=0),
    )(place, tokens, got, mine, theirs, weights)


def split_kernel(both, u, weights):
    total = both[0, :512].astype(F32)
    for k in range(1, 8):
        total += both[k, :512].astype(F32)
    u[...] = total.astype(BF16)
    for k in range(8):
        weights[k] = both[k, 512:]


def split_sum(both):
    vmem = pl.BlockSpec(memory_space=pltpu.VMEM)
    return pl.pallas_call(
        split_kernel,
        in_specs=[vmem],
        out_specs=[vmem, vmem],
        out_shape=[jax.ShapeDtypeStruct((512, 256), BF16), jax.ShapeDtypeStruct((8, 256, 256), BF16)],
        compiler_params=pltpu.CompilerParams(vmem_limit_bytes=8 << 20),
        cost_estimate=pl.CostEstimate(flops=1 << 20, bytes_accessed=5 << 20, transcendentals=0),
    )(both)


def weight_pieces(place, half, refs):
    pieces = []
    for block in range(8):
        for ref, side in zip(refs, (place[0], 1 - place[0])):
            start = pl.multiple_of(512 * (8 * half + block) + 256 * side, 256)
            pieces.append((ref, 32 * block, start))
    return pieces


def project(tokens, pieces, total):
    for ref, row, start in pieces:
        w = ref[:, row : row + 32].reshape(256, 256)
        total += jnp.dot(tokens[:, pl.ds(start, 256)], w, preferred_element_type=F32)
    return total


def first_kernel(place, tokens, w0, w1, out):
    out[...] = project(tokens, weight_pieces(place, place[1], (w0, w1)), jnp.zeros(out.shape, F32))


def first_half(place, tokens, weights):
    vmem = pl.BlockSpec(memory_space=pltpu.VMEM)
    return pl.pallas_call(
        first_kernel,
        in_specs=[pl.BlockSpec(memory_space=pltpu.SMEM)] + [vmem] * 3,
        out_specs=vmem,
        out_shape=jax.ShapeDtypeStruct((tokens.shape[0], 256), F32),
        compiler_params=pltpu.CompilerParams(vmem_limit_bytes=8 << 20),
        cost_estimate=pl.CostEstimate(flops=1 << 20, bytes_accessed=1 << 10, transcendentals=0),
    )(place, tokens, *weights)


def final_kernel(place, tokens, cot, inv, kv_half, w0, w1, w2, w3, kv_out, token_grad):
    width = tokens.shape[1]
    later = weight_pieces(place, 1 - place[1], (w2, w3))
    root = inv[:, :1]
    kv = project(tokens, later, kv_half[...]) * root
    kv_out[...] = kv.astype(BF16)
    g = cot[...]
    slopes = jnp.sum(g.astype(F32) * kv, -1, keepdims=True) * (1.0 / width)
    slopes = root * slopes
    for ref, row, start in weight_pieces(place, place[1], (w0, w1)) + later:
        w = ref[:, row : row + 32].reshape(256, 256)
        back = lax.dot_general(g, w, (((1,), (1,)), ((), ())), preferred_element_type=F32)
        x = tokens[:, pl.ds(start, 256)].astype(F32)
        token_grad[:, pl.ds(start, 256)] = (root * (back - x * slopes)).astype(BF16)


def final(place, tokens, cot, inv, kv_half, weights):
    vmem = pl.BlockSpec(memory_space=pltpu.VMEM)
    return pl.pallas_call(
        final_kernel,
        in_specs=[pl.BlockSpec(memory_space=pltpu.SMEM)] + [vmem] * 8,
        out_specs=[vmem, vmem],
        out_shape=[
            jax.ShapeDtypeStruct(cot.shape, BF16),
            jax.ShapeDtypeStruct(tokens.shape, BF16),
        ],
        compiler_params=pltpu.CompilerParams(vmem_limit_bytes=14 << 20),
        cost_estimate=pl.CostEstimate(flops=1 << 20, bytes_accessed=1 << 10, transcendentals=0),
    )(place, tokens, cot, inv, kv_half, *weights)


def total_kernel(parts, out):
    total = parts[0].astype(F32)
    for k in range(1, parts.shape[0]):
        total += parts[k].astype(F32)
    out[...] = total * (1.0 / 256.0)


def total_of(parts):
    vmem = pl.BlockSpec(memory_space=pltpu.VMEM)
    return pl.pallas_call(
        total_kernel,
        in_specs=[vmem],
        out_specs=vmem,
        out_shape=jax.ShapeDtypeStruct(parts.shape[1:], F32),
        compiler_params=pltpu.CompilerParams(vmem_limit_bytes=2 << 20),
        cost_estimate=pl.CostEstimate(flops=50 * 10**9, bytes_accessed=1 << 18, transcendentals=0),
    )(parts)


SWAP = [(0, 1), (1, 0)]


def cubes():
    index = np.arange(math.prod(SIZES)).reshape(SIZES)
    groups = []
    for core in range(2):
        for x0, y0, z0 in itertools.product(range(core, 4, 2), range(core, 8, 2), range(core, 8, 2)):
            members = {}
            for a, b, c in itertools.product(range(2), repeat=3):
                x, y, z = (x0 + a) % 4, (y0 + b) % 8, (z0 + c) % 8
                members[x % 2, y % 2, z % 2] = int(index[x // 2, y // 2, y % 2, core, z // 2, z % 2, x % 2])
            groups.append([members[k] for k in sorted(members)])
    return groups


ALONG_X = [
    (4 * (x // 2) + 2 * c + x % 2, 4 * ((x ^ (1 + 2 * c)) // 2) + 2 * c + 1 - x % 2)
    for c in range(2)
    for x in range(4)
]


def body(tokens, cotangent, kv_weight, norm_gain):
    xl, zl = lax.axis_index("xl"), lax.axis_index("zl")
    place = jnp.stack([lax.axis_index("c"), xl, zl]).astype(jnp.int32)
    piece = 4 * lax.axis_index("zh") + 2 * zl + xl

    share = make_share(place, kv_weight, norm_gain.reshape(1, 256))
    share = lax.all_to_all(share, ("xh", "yh", "yl"), 0, 0, tiled=True).reshape(512, 256)

    got = lax.ppermute(tokens, "c", SWAP)
    scaled, inv = prep(tokens, cotangent)
    got_scaled = lax.ppermute(scaled, "c", SWAP)

    both = merge(place, tokens, got, scaled, got_scaled, share)
    both = lax.all_to_all(both, AXES, 0, 0, tiled=True, axis_index_groups=cubes())
    u, w0 = split_sum(both)

    w2 = lax.ppermute(w0, ("xh", "c", "xl"), ALONG_X)
    w1 = lax.ppermute(w0, "c", SWAP)
    kv_half = first_half(place, tokens, (w0, w1))
    w2, kv_half = lax.optimization_barrier((w2, kv_half))
    w3 = lax.ppermute(w2, "c", SWAP)

    u = lax.all_to_all(u.reshape(32, 16, 256), ("xh", "yh", "zh"), 0, 0, tiled=True)
    u, w3 = lax.optimization_barrier((total_of(u), w3))
    kv_out, token_grad = final(place, tokens, cotangent, inv, kv_half, (w0, w1, w2, w3))
    gain = lax.dynamic_slice_in_dim(norm_gain, 16 * piece, 16, 0).astype(F32)[:, None]
    rows = lax.dynamic_slice_in_dim(kv_weight, 16 * piece, 16, 0).astype(F32)
    kv_grad = (u * gain).astype(BF16)
    gain_grad = jnp.sum(u * rows, -1).astype(BF16)
    return (kv_out, token_grad, kv_grad, gain_grad)


def solution(mesh):
    split = Mesh(mesh.devices.reshape(SIZES), AXES)
    every, inner = P(AXES, None), ("xh", "yh", "yl", "c")
    return jax.shard_map(
        body,
        mesh=split,
        in_specs=(every, every, P(inner, None), P(inner)),
        out_specs=(every, every, every, P(AXES)),
        check_vma=False,
    )
```

```python
import itertools
import math

import jax
import jax.numpy as jnp
import numpy as np
from jax import lax
from jax.experimental import pallas as pl
from jax.experimental.pallas import tpu as pltpu
from jax.sharding import Mesh, PartitionSpec as P

AXES = ("xh", "yh", "yl", "c", "zh", "zl", "xl")
SIZES = (2, 4, 2, 2, 4, 2, 2)
F32, BF16 = jnp.float32, jnp.bfloat16


def share_kernel(place, weight, gain, out, scaled):
    xl, zl = place[1], place[3]
    row = lax.broadcasted_iota(jnp.int32, (256, 256), 0)
    column = lax.broadcasted_iota(jnp.int32, (256, 256), 1)
    diagonal = jnp.where(row == column, gain[...].astype(F32).reshape(1, 256), 0.0).astype(BF16)
    scaled[...] = jnp.dot(diagonal, weight[...], preferred_element_type=F32).astype(BF16)
    for yl in range(2):
        rows = scaled[pl.ds(pl.multiple_of(128 * xl + 64 * yl + 32 * zl, 32), 32), :]
        for k in range(8):
            out[2 * k + yl] = rows


def make_share(place, weight, gain):
    vmem = pl.BlockSpec(memory_space=pltpu.VMEM)
    return pl.pallas_call(
        share_kernel,
        in_specs=[pl.BlockSpec(memory_space=pltpu.SMEM), vmem, vmem],
        out_specs=vmem,
        out_shape=jax.ShapeDtypeStruct((16, 32, 256), BF16),
        scratch_shapes=[pltpu.VMEM((256, 256), BF16)],
        compiler_params=pltpu.CompilerParams(vmem_limit_bytes=4 << 20),
        cost_estimate=pl.CostEstimate(flops=1 << 25, bytes_accessed=1 << 19, transcendentals=0),
    )(place, weight, gain)


def roots(tokens):
    wide = tokens[...].astype(F32)
    return lax.rsqrt(jnp.mean(wide * wide, -1, keepdims=True) + 1e-05)


def outer_kernel(core, tokens, got, cot, got_cot, out, inv):
    mine, theirs = roots(tokens), roots(got)
    inv[...] = jnp.broadcast_to(mine, inv.shape)
    right = jnp.concatenate([cot[...].astype(F32) * mine, got_cot[...].astype(F32) * theirs], 0).astype(BF16)
    for xh in range(2):
        for yh in range(4):
            for yl in range(2):
                block = 8 * xh + 2 * yh + yl
                start = pl.multiple_of(512 * block + 256 * core[0], 256)
                left = jnp.concatenate([tokens[:, pl.ds(start, 256)], got[:, pl.ds(start, 256)]], 0)
                u = lax.dot_general(left, right, (((0,), (0,)), ((), ())), preferred_element_type=F32)
                u = u.reshape(4, 2, 2, 16, 256).astype(BF16)
                first = 64 * (4 * xh + yh)
                for xl in range(2):
                    for zl in range(2):
                        out[4 * xl + 2 * yl + zl, first : first + 64] = u[:, zl, xl].reshape(64, 256)


def outer_terms(core, tokens, got, cot, got_cot):
    vmem = pl.BlockSpec(memory_space=pltpu.VMEM)
    return pl.pallas_call(
        outer_kernel,
        in_specs=[pl.BlockSpec(memory_space=pltpu.SMEM)] + [vmem] * 4,
        out_specs=[vmem, vmem],
        out_shape=[
            jax.ShapeDtypeStruct((8, 512, 256), BF16),
            jax.ShapeDtypeStruct((tokens.shape[0], 128), F32),
        ],
        compiler_params=pltpu.CompilerParams(vmem_limit_bytes=12 << 20),
        cost_estimate=pl.CostEstimate(flops=2 * tokens.size * 256, bytes_accessed=8 * tokens.size, transcendentals=0),
    )(core, tokens, got, cot, got_cot)


def sum_kernel(parts, out, after):
    after[...] = jnp.zeros_like(after)
    total = parts[0].astype(F32)
    for k in range(1, 8):
        total += parts[k].astype(F32)
    out[...] = total.astype(BF16)


def sum_of(parts):
    vmem = pl.BlockSpec(memory_space=pltpu.VMEM)
    return pl.pallas_call(
        sum_kernel,
        in_specs=[vmem],
        out_specs=[vmem, vmem],
        out_shape=[jax.ShapeDtypeStruct(parts.shape[1:], BF16), jax.ShapeDtypeStruct((8, 128), F32)],
        compiler_params=pltpu.CompilerParams(vmem_limit_bytes=8 << 20),
        cost_estimate=pl.CostEstimate(flops=1 << 20, bytes_accessed=2 << 20, transcendentals=0),
    )(parts)


def weight_pieces(place, half, refs):
    yl, zl = place[2], place[3]

    def reader(ref, row):
        return lambda: jnp.concatenate(
            [ref[2 * (sz + zl - 2 * sz * zl) + (sy + yl - 2 * sy * yl), row : row + 32] for sy in range(2) for sz in range(2)], 0
        )

    pieces = []
    for block in range(16):
        for ref, side in zip(refs, (place[0], 1 - place[0])):
            start = pl.multiple_of(512 * block + 256 * side + 128 * half, 128)
            pieces.append((reader(ref, 32 * block), start))
    return pieces


def project(tokens, pieces, total):
    for read, start in pieces:
        total += jnp.dot(tokens[:, pl.ds(start, 128)], read(), preferred_element_type=F32)
    return total


def first_kernel(place, tokens, w0, w1, out):
    out[...] = project(tokens, weight_pieces(place, place[1], (w0, w1)), jnp.zeros(out.shape, F32))


def first_half(place, tokens, weights):
    vmem = pl.BlockSpec(memory_space=pltpu.VMEM)
    return pl.pallas_call(
        first_kernel,
        in_specs=[pl.BlockSpec(memory_space=pltpu.SMEM)] + [vmem] * 3,
        out_specs=vmem,
        out_shape=jax.ShapeDtypeStruct((tokens.shape[0], 256), F32),
        compiler_params=pltpu.CompilerParams(vmem_limit_bytes=8 << 20),
        cost_estimate=pl.CostEstimate(flops=1 << 20, bytes_accessed=1 << 10, transcendentals=0),
    )(place, tokens, *weights)


def final_kernel(place, tokens, cot, inv, kv_half, w0, w1, w2, w3, kv_out, token_grad):
    width = tokens.shape[1]
    later = weight_pieces(place, 1 - place[1], (w2, w3))
    root = inv[:, :1]
    kv = project(tokens, later, kv_half[...]) * root
    kv_out[...] = kv.astype(BF16)
    g = cot[...]
    slopes = jnp.sum(g.astype(F32) * kv, -1, keepdims=True) * (1.0 / width)
    slopes = root * slopes
    for read, start in weight_pieces(place, place[1], (w0, w1)) + later:
        back = lax.dot_general(g, read(), (((1,), (1,)), ((), ())), preferred_element_type=F32)
        x = tokens[:, pl.ds(start, 128)].astype(F32)
        token_grad[:, pl.ds(start, 128)] = (root * (back - x * slopes)).astype(BF16)


def final(place, tokens, cot, inv, kv_half, weights):
    vmem = pl.BlockSpec(memory_space=pltpu.VMEM)
    return pl.pallas_call(
        final_kernel,
        in_specs=[pl.BlockSpec(memory_space=pltpu.SMEM)] + [vmem] * 8,
        out_specs=[vmem, vmem],
        out_shape=[
            jax.ShapeDtypeStruct(cot.shape, BF16),
            jax.ShapeDtypeStruct(tokens.shape, BF16),
        ],
        compiler_params=pltpu.CompilerParams(vmem_limit_bytes=14 << 20),
        cost_estimate=pl.CostEstimate(flops=1 << 20, bytes_accessed=1 << 10, transcendentals=0),
    )(place, tokens, cot, inv, kv_half, *weights)


def total_kernel(parts, out):
    total = parts[0].astype(F32)
    for k in range(1, parts.shape[0]):
        total += parts[k].astype(F32)
    out[...] = total * (1.0 / 256.0)


def total_of(parts):
    vmem = pl.BlockSpec(memory_space=pltpu.VMEM)
    return pl.pallas_call(
        total_kernel,
        in_specs=[vmem],
        out_specs=vmem,
        out_shape=jax.ShapeDtypeStruct(parts.shape[1:], F32),
        compiler_params=pltpu.CompilerParams(vmem_limit_bytes=2 << 20),
        cost_estimate=pl.CostEstimate(flops=50 * 10**9, bytes_accessed=1 << 18, transcendentals=0),
    )(parts)


SWAP = [(0, 1), (1, 0)]


def cubes():
    index = np.arange(math.prod(SIZES)).reshape(SIZES)
    groups = []
    for core in range(2):
        for x0, y0, z0 in itertools.product(range(core, 4, 2), range(core, 8, 2), range(core, 8, 2)):
            members = {}
            for a, b, c in itertools.product(range(2), repeat=3):
                x, y, z = (x0 + a) % 4, (y0 + b) % 8, (z0 + c) % 8
                members[x % 2, y % 2, z % 2] = int(index[x // 2, y // 2, y % 2, core, z // 2, z % 2, x % 2])
            groups.append([members[k] for k in sorted(members)])
    return groups


def neighbours(axis):
    count = 4 if axis == "x" else 8

    def place(at, core):
        high, low = at // 2, at % 2
        if axis == "x":
            return 4 * high + 2 * core + low
        if axis == "y":
            return 4 * high + 2 * low + core
        return 8 * core + at

    return [
        (place(at, core), place((at + (1 if at % 2 == core else -1)) % count, core))
        for core in range(2)
        for at in range(count)
    ]


def body(tokens, cotangent, kv_weight, norm_gain):
    yl, xl, zl = lax.axis_index("yl"), lax.axis_index("xl"), lax.axis_index("zl")
    place = jnp.stack([lax.axis_index("c"), xl, yl, zl]).astype(jnp.int32)
    piece = 4 * lax.axis_index("zh") + 2 * zl + xl

    share = make_share(place, kv_weight, norm_gain)
    share = lax.all_to_all(share, ("xh", "yh", "yl"), 0, 0, tiled=True).reshape(1, 512, 256)

    got, got_cotangent = lax.ppermute(tokens, "c", SWAP), lax.ppermute(cotangent, "c", SWAP)
    u, inv = outer_terms(place, tokens, got, cotangent, got_cotangent)
    u, after = sum_of(lax.all_to_all(u, AXES, 0, 0, tiled=True, axis_index_groups=cubes()))
    u = lax.all_to_all(u.reshape(32, 16, 256), ("xh", "yh", "zh"), 0, 0, tiled=True)

    share = jnp.concatenate([share, lax.ppermute(share, ("yh", "yl", "c"), neighbours("y"))])
    w0 = jnp.concatenate([share, lax.ppermute(share, ("c", "zh", "zl"), neighbours("z"))])
    w2 = lax.ppermute(w0, ("xh", "c", "xl"), neighbours("x"))
    w1 = lax.ppermute(w0, "c", SWAP)
    kv_half = first_half(place, tokens, (w0, w1))
    w2, kv_half = lax.optimization_barrier((w2, kv_half))
    w3 = lax.ppermute(w2, "c", SWAP)
    u, w3 = lax.optimization_barrier((total_of(u), w3))
    kv_out, token_grad = final(place, tokens, cotangent, inv, kv_half, (w0, w1, w2, w3))

    gain = lax.dynamic_slice_in_dim(norm_gain, 16 * piece, 16, 0).astype(F32)[:, None]
    rows = lax.dynamic_slice_in_dim(kv_weight, 16 * piece, 16, 0).astype(F32)
    kv_grad = (u * gain).astype(BF16)
    gain_grad = jnp.sum(u * rows, -1).astype(BF16)
    return (kv_out, token_grad, kv_grad, gain_grad)


def solution(mesh):
    split = Mesh(mesh.devices.reshape(SIZES), AXES)
    every, inner = P(AXES, None), ("xh", "yh", "yl", "c")
    return jax.shard_map(
        body,
        mesh=split,
        in_specs=(every, every, P(inner, None), P(inner)),
        out_specs=(every, every, every, P(AXES)),
        check_vma=False,
    )
```

```python
import itertools
import math

import jax
import jax.numpy as jnp
import numpy as np
from jax import lax
from jax.experimental import pallas as pl
from jax.experimental.pallas import tpu as pltpu
from jax.sharding import Mesh, PartitionSpec as P

AXES = ("xh", "yh", "yl", "c", "zh", "zl", "xl")
SIZES = (2, 4, 2, 2, 4, 2, 2)
F32, BF16 = jnp.float32, jnp.bfloat16


def share_kernel(place, weight, gain, out, held, held_gain, scaled, sems):
    xl, zl = place[1], place[2]
    fetches = [
        pltpu.make_async_copy(weight, held, sems.at[0]),
        pltpu.make_async_copy(gain, held_gain, sems.at[1]),
    ]
    for fetch in fetches:
        fetch.start()
    row = lax.broadcasted_iota(jnp.int32, (256, 256), 0)
    column = lax.broadcasted_iota(jnp.int32, (256, 256), 1)
    for fetch in fetches:
        fetch.wait()
    diagonal = jnp.where(row == column, held_gain[...].astype(F32).reshape(1, 256), 0.0).astype(BF16)
    scaled[...] = jnp.dot(diagonal, held[...], preferred_element_type=F32).astype(BF16)
    for yl in range(2):
        rows = scaled[pl.ds(pl.multiple_of(128 * xl + 64 * yl + 32 * zl, 32), 32), :]
        for k in range(8):
            out[2 * k + yl] = rows


def make_share(place, weight, gain):
    main = pl.BlockSpec(memory_space=pltpu.HBM)
    return pl.pallas_call(
        share_kernel,
        in_specs=[pl.BlockSpec(memory_space=pltpu.SMEM), main, main],
        out_specs=pl.BlockSpec(memory_space=pltpu.VMEM),
        out_shape=jax.ShapeDtypeStruct((16, 32, 256), BF16),
        scratch_shapes=[
            pltpu.VMEM((256, 256), BF16),
            pltpu.VMEM((256,), BF16),
            pltpu.VMEM((256, 256), BF16),
            pltpu.SemaphoreType.DMA((2,)),
        ],
        compiler_params=pltpu.CompilerParams(vmem_limit_bytes=4 << 20),
        cost_estimate=pl.CostEstimate(flops=1 << 25, bytes_accessed=1 << 19, transcendentals=0),
    )(place, weight, gain)


def roots(tokens):
    wide = tokens[...].astype(F32)
    return lax.rsqrt(jnp.mean(wide * wide, -1, keepdims=True) + 1e-05)


def outer_kernel(core, tokens, got, cot, got_cot, out, inv):
    mine, theirs = roots(tokens), roots(got)
    inv[...] = jnp.broadcast_to(mine, inv.shape)
    right = jnp.concatenate([cot[...].astype(F32) * mine, got_cot[...].astype(F32) * theirs], 0).astype(BF16)
    for xh in range(2):
        for yh in range(4):
            for yl in range(2):
                block = 8 * xh + 2 * yh + yl
                start = pl.multiple_of(512 * block + 256 * core[0], 256)
                left = jnp.concatenate([tokens[:, pl.ds(start, 256)], got[:, pl.ds(start, 256)]], 0)
                u = lax.dot_general(left, right, (((0,), (0,)), ((), ())), preferred_element_type=F32)
                u = u.reshape(4, 2, 2, 16, 256).astype(BF16)
                first = 64 * (4 * xh + yh)
                for xl in range(2):
                    for zl in range(2):
                        out[4 * xl + 2 * yl + zl, first : first + 64] = u[:, zl, xl].reshape(64, 256)


def outer_terms(core, tokens, got, cot, got_cot):
    vmem = pl.BlockSpec(memory_space=pltpu.VMEM)
    return pl.pallas_call(
        outer_kernel,
        in_specs=[pl.BlockSpec(memory_space=pltpu.SMEM)] + [vmem] * 4,
        out_specs=[vmem, vmem],
        out_shape=[
            jax.ShapeDtypeStruct((8, 1024, 256), BF16),
            jax.ShapeDtypeStruct((tokens.shape[0], 128), F32),
        ],
        compiler_params=pltpu.CompilerParams(vmem_limit_bytes=12 << 20),
        cost_estimate=pl.CostEstimate(flops=2 * tokens.size * 256, bytes_accessed=8 * tokens.size, transcendentals=0),
    )(core, tokens, got, cot, got_cot)


def split_kernel(both, u, weights):
    total = both[0, :512].astype(F32)
    for k in range(1, 8):
        total += both[k, :512].astype(F32)
    u[...] = total.astype(BF16)
    for k in range(8):
        weights[k] = both[k, 512:]


def split_sum(both):
    vmem = pl.BlockSpec(memory_space=pltpu.VMEM)
    return pl.pallas_call(
        split_kernel,
        in_specs=[vmem],
        out_specs=[vmem, vmem],
        out_shape=[jax.ShapeDtypeStruct((512, 256), BF16), jax.ShapeDtypeStruct((8, 512, 256), BF16)],
        compiler_params=pltpu.CompilerParams(vmem_limit_bytes=10 << 20),
        cost_estimate=pl.CostEstimate(flops=1 << 20, bytes_accessed=6 << 20, transcendentals=0),
    )(both)


def final_kernel(place, tokens, cot, inv, w_mine, w_theirs, kv_out, token_grad):
    rows, width = tokens.shape
    pieces = []
    for block in range(16):
        for ref, side in ((w_mine, place[0]), (w_theirs, 1 - place[0])):
            pieces.append((ref, 32 * block, pl.multiple_of(512 * block + 256 * side, 256)))
    total = jnp.zeros((rows, 256), F32)
    for ref, row, start in pieces:
        w = ref[:, row : row + 32].reshape(256, 256)
        total += jnp.dot(tokens[:, pl.ds(start, 256)], w, preferred_element_type=F32)
    root = inv[:, :1]
    kv = total * root
    kv_out[...] = kv.astype(BF16)
    g = cot[...]
    slopes = jnp.sum(g.astype(F32) * kv, -1, keepdims=True) * (1.0 / width)
    slopes = root * slopes
    for ref, row, start in pieces:
        w = ref[:, row : row + 32].reshape(256, 256)
        back = lax.dot_general(g, w, (((1,), (1,)), ((), ())), preferred_element_type=F32)
        x = tokens[:, pl.ds(start, 256)].astype(F32)
        token_grad[:, pl.ds(start, 256)] = (root * (back - x * slopes)).astype(BF16)


def final(place, tokens, cot, inv, w_mine, w_theirs):
    vmem = pl.BlockSpec(memory_space=pltpu.VMEM)
    return pl.pallas_call(
        final_kernel,
        in_specs=[pl.BlockSpec(memory_space=pltpu.SMEM)] + [vmem] * 5,
        out_specs=[vmem, vmem],
        out_shape=[
            jax.ShapeDtypeStruct(cot.shape, BF16),
            jax.ShapeDtypeStruct(tokens.shape, BF16),
        ],
        compiler_params=pltpu.CompilerParams(vmem_limit_bytes=14 << 20),
        cost_estimate=pl.CostEstimate(flops=4 * tokens.size * 256, bytes_accessed=8 << 20, transcendentals=0),
    )(place, tokens, cot, inv, w_mine, w_theirs)


def finish_kernel(parts, rows, gain, kv_grad, gain_grad):
    u = parts[0].astype(F32)
    for k in range(1, parts.shape[0]):
        u += parts[k].astype(F32)
    u = u * (1.0 / 256.0)
    size = u.shape[0]
    diagonal = lax.broadcasted_iota(jnp.int32, (size, size), 0) == lax.broadcasted_iota(jnp.int32, (size, size), 1)
    column = jnp.sum(jnp.where(diagonal, gain[...].astype(F32).reshape(1, size), 0.0), 1, keepdims=True)
    kv_grad[...] = (u * column).astype(BF16)
    sums = jnp.sum(u * rows[...].astype(F32), 1, keepdims=True)
    gain_grad[...] = jnp.sum(jnp.where(diagonal, sums, 0.0), 0).astype(BF16)


def finish(parts, rows, gain):
    vmem = pl.BlockSpec(memory_space=pltpu.VMEM)
    return pl.pallas_call(
        finish_kernel,
        in_specs=[vmem] * 3,
        out_specs=[vmem, vmem],
        out_shape=[jax.ShapeDtypeStruct(rows.shape, BF16), jax.ShapeDtypeStruct(gain.shape, BF16)],
        compiler_params=pltpu.CompilerParams(vmem_limit_bytes=2 << 20),
        cost_estimate=pl.CostEstimate(flops=1 << 20, bytes_accessed=1 << 18, transcendentals=0),
    )(parts, rows, gain)


SWAP = [(0, 1), (1, 0)]


def cubes():
    index = np.arange(math.prod(SIZES)).reshape(SIZES)
    groups = []
    for core in range(2):
        for x0, y0, z0 in itertools.product(range(core, 4, 2), range(core, 8, 2), range(core, 8, 2)):
            members = {}
            for a, b, c in itertools.product(range(2), repeat=3):
                x, y, z = (x0 + a) % 4, (y0 + b) % 8, (z0 + c) % 8
                members[x % 2, y % 2, z % 2] = int(index[x // 2, y // 2, y % 2, core, z // 2, z % 2, x % 2])
            groups.append([members[k] for k in sorted(members)])
    return groups


def body(tokens, cotangent, kv_weight, norm_gain):
    xl, zl = lax.axis_index("xl"), lax.axis_index("zl")
    place = jnp.stack([lax.axis_index("c"), xl, zl]).astype(jnp.int32)
    piece = 4 * lax.axis_index("zh") + 2 * zl + xl

    share = make_share(place, kv_weight, norm_gain)
    share = lax.all_to_all(share, ("xh", "yh", "yl"), 0, 0, tiled=True).reshape(512, 256)

    got, got_cotangent = lax.ppermute(tokens, "c", SWAP), lax.ppermute(cotangent, "c", SWAP)
    both, inv = outer_terms(place, tokens, got, cotangent, got_cotangent)

    both = lax.dynamic_update_slice(both, jnp.broadcast_to(share, (8, 512, 256)), (0, 512, 0))
    both = lax.all_to_all(both, AXES, 0, 0, tiled=True, axis_index_groups=cubes())
    u, w_mine = split_sum(both)
    w_theirs = lax.ppermute(w_mine, "c", SWAP)

    u = lax.all_to_all(u.reshape(32, 16, 256), ("xh", "yh", "zh"), 0, 0, tiled=True)
    kv_out, token_grad = final(place, tokens, cotangent, inv, w_mine, w_theirs)
    gain = lax.dynamic_slice_in_dim(norm_gain, 16 * piece, 16, 0)
    rows = lax.dynamic_slice_in_dim(kv_weight, 16 * piece, 16, 0)
    u, kv_out, gain, rows = lax.optimization_barrier((u, kv_out, gain, rows))
    kv_grad, gain_grad = finish(u, rows, gain)
    return (kv_out, token_grad, kv_grad, gain_grad)


def solution(mesh):
    split = Mesh(mesh.devices.reshape(SIZES), AXES)
    every, inner = P(AXES, None), ("xh", "yh", "yl", "c")
    return jax.shard_map(
        body,
        mesh=split,
        in_specs=(every, every, P(inner, None), P(inner)),
        out_specs=(every, every, every, P(AXES)),
        check_vma=False,
    )
```

```python
import itertools
import math

import jax
import jax.numpy as jnp
import numpy as np
from jax import lax
from jax.experimental import pallas as pl
from jax.experimental.pallas import tpu as pltpu
from jax.sharding import Mesh, PartitionSpec as P

AXES = ("xh", "yh", "yl", "c", "zh", "zl", "xl")
SIZES = (2, 4, 2, 2, 4, 2, 2)
F32, BF16 = jnp.float32, jnp.bfloat16


def share_kernel(place, weight, gain, out, held, held_gain, scaled, sems):
    xl, zl = place[1], place[2]
    fetches = [
        pltpu.make_async_copy(weight, held, sems.at[0]),
        pltpu.make_async_copy(gain, held_gain, sems.at[1]),
    ]
    for fetch in fetches:
        fetch.start()
    row = lax.broadcasted_iota(jnp.int32, (256, 256), 0)
    column = lax.broadcasted_iota(jnp.int32, (256, 256), 1)
    for fetch in fetches:
        fetch.wait()
    diagonal = jnp.where(row == column, held_gain[...].astype(F32).reshape(1, 256), 0.0).astype(BF16)
    scaled[...] = jnp.dot(diagonal, held[...], preferred_element_type=F32).astype(BF16)
    for yl in range(2):
        rows = scaled[pl.ds(pl.multiple_of(128 * xl + 64 * yl + 32 * zl, 32), 32), :]
        for k in range(8):
            out[2 * k + yl] = rows


def make_share(place, weight, gain):
    main = pl.BlockSpec(memory_space=pltpu.HBM)
    return pl.pallas_call(
        share_kernel,
        in_specs=[pl.BlockSpec(memory_space=pltpu.SMEM), main, main],
        out_specs=pl.BlockSpec(memory_space=pltpu.VMEM),
        out_shape=jax.ShapeDtypeStruct((16, 32, 256), BF16),
        scratch_shapes=[
            pltpu.VMEM((256, 256), BF16),
            pltpu.VMEM((256,), BF16),
            pltpu.VMEM((256, 256), BF16),
            pltpu.SemaphoreType.DMA((2,)),
        ],
        compiler_params=pltpu.CompilerParams(vmem_limit_bytes=4 << 20),
        cost_estimate=pl.CostEstimate(flops=1 << 25, bytes_accessed=1 << 19, transcendentals=0),
    )(place, weight, gain)


def outer_kernel(place, tokens, got, cot, got_cot, out, inv, held, stage, in_sems, out_sems):
    width = held.shape[2]
    chunk = width // 4
    fetches = [
        [
            pltpu.make_async_copy(source.at[:, pl.ds(chunk * q, chunk)], held.at[k, :, pl.ds(chunk * q, chunk)], in_sems.at[k, q])
            for k, source in enumerate((tokens, got))
        ]
        for q in range(4)
    ]
    for pair in fetches:
        for fetch in pair:
            fetch.start()
    squares = [jnp.zeros((held.shape[1], 1), F32) for _ in range(2)]
    for q, pair in enumerate(fetches):
        for k, fetch in enumerate(pair):
            fetch.wait()
            wide = held[k, :, chunk * q : chunk * (q + 1)].astype(F32)
            squares[k] += jnp.sum(wide * wide, -1, keepdims=True)
    mine, theirs = (lax.rsqrt(total * (1.0 / width) + 1e-05) for total in squares)
    inv[...] = jnp.broadcast_to(mine, inv.shape)
    right = jnp.concatenate([cot[...].astype(F32) * mine, got_cot[...].astype(F32) * theirs], 0).astype(BF16)
    stores = []
    for yl in range(2):
        for xh in range(2):
            for yh in range(4):
                block = 8 * xh + 2 * yh + yl
                start = pl.multiple_of(512 * block + 256 * place[0], 256)
                left = jnp.concatenate([held[k, :, pl.ds(start, 256)] for k in range(2)], 0)
                u = lax.dot_general(left, right, (((0,), (0,)), ((), ())), preferred_element_type=F32)
                u = u.reshape(4, 2, 2, 16, 256).astype(BF16)
                first = 64 * (4 * xh + yh)
                for xl in range(2):
                    for zl in range(2):
                        stage[4 * xl + 2 * yl + zl, first : first + 64] = u[:, zl, xl].reshape(64, 256)
        for k in (2 * yl, 2 * yl + 1, 4 + 2 * yl, 5 + 2 * yl):
            store = pltpu.make_async_copy(stage.at[k], out.at[k, pl.ds(0, 512)], out_sems.at[k])
            store.start()
            stores.append(store)
    for store in stores:
        store.wait()


def outer_terms(place, tokens, got, cot, got_cot):
    vmem, anywhere = pl.BlockSpec(memory_space=pltpu.VMEM), pl.BlockSpec(memory_space=pl.ANY)
    rows, width = tokens.shape
    return pl.pallas_call(
        outer_kernel,
        in_specs=[pl.BlockSpec(memory_space=pltpu.SMEM), anywhere, anywhere, vmem, vmem],
        out_specs=[anywhere, vmem],
        out_shape=[
            jax.ShapeDtypeStruct((8, 1024, 256), BF16),
            jax.ShapeDtypeStruct((rows, 128), F32),
        ],
        scratch_shapes=[
            pltpu.VMEM((2, rows, width), BF16),
            pltpu.VMEM((8, 512, 256), BF16),
            pltpu.SemaphoreType.DMA((2, 4)),
            pltpu.SemaphoreType.DMA((8,)),
        ],
        compiler_params=pltpu.CompilerParams(vmem_limit_bytes=62 << 20),
        cost_estimate=pl.CostEstimate(flops=2 * tokens.size * 256, bytes_accessed=8 * tokens.size, transcendentals=0),
    )(place, tokens, got, cot, got_cot)


def sum_kernel(both, out):
    total = both[0].astype(F32)
    for k in range(1, 8):
        total += both[k].astype(F32)
    out[...] = total.astype(BF16)


def sum_of(both):
    return pl.pallas_call(
        sum_kernel,
        grid=(1,),
        in_specs=[pl.BlockSpec((8, 512, 256), lambda i: (0, 0, 0))],
        out_specs=pl.BlockSpec((512, 256), lambda i: (0, 0)),
        out_shape=jax.ShapeDtypeStruct((512, 256), BF16),
        compiler_params=pltpu.CompilerParams(vmem_limit_bytes=8 << 20),
        cost_estimate=pl.CostEstimate(flops=1 << 20, bytes_accessed=2 << 20, transcendentals=0),
    )(both)


def final_kernel(place, tokens, cot, inv, w_mine, w_theirs, kv_out, token_grad):
    rows, width = tokens.shape
    pieces = []
    for block in range(16):
        for ref, side in ((w_mine, place[0]), (w_theirs, 1 - place[0])):
            pieces.append((ref, 32 * block, pl.multiple_of(512 * block + 256 * side, 256)))
    total = jnp.zeros((rows, 256), F32)
    for ref, row, start in pieces:
        w = ref[:, 512 + row : 544 + row].reshape(256, 256)
        total += jnp.dot(tokens[:, pl.ds(start, 256)], w, preferred_element_type=F32)
    root = inv[:, :1]
    kv = total * root
    kv_out[...] = kv.astype(BF16)
    g = cot[...]
    slopes = jnp.sum(g.astype(F32) * kv, -1, keepdims=True) * (1.0 / width)
    slopes = root * slopes
    for ref, row, start in pieces:
        w = ref[:, 512 + row : 544 + row].reshape(256, 256)
        back = lax.dot_general(g, w, (((1,), (1,)), ((), ())), preferred_element_type=F32)
        x = tokens[:, pl.ds(start, 256)].astype(F32)
        token_grad[:, pl.ds(start, 256)] = (root * (back - x * slopes)).astype(BF16)


def final(place, tokens, cot, inv, w_mine, w_theirs):
    vmem = pl.BlockSpec(memory_space=pltpu.VMEM)
    return pl.pallas_call(
        final_kernel,
        in_specs=[pl.BlockSpec(memory_space=pltpu.SMEM)] + [vmem] * 5,
        out_specs=[vmem, vmem],
        out_shape=[
            jax.ShapeDtypeStruct(cot.shape, BF16),
            jax.ShapeDtypeStruct(tokens.shape, BF16),
        ],
        compiler_params=pltpu.CompilerParams(vmem_limit_bytes=14 << 20),
        cost_estimate=pl.CostEstimate(flops=4 * tokens.size * 256, bytes_accessed=8 << 20, transcendentals=0),
    )(place, tokens, cot, inv, w_mine, w_theirs)


def finish_kernel(parts, rows, gain, kv_grad, gain_grad):
    u = parts[0].astype(F32)
    for k in range(1, parts.shape[0]):
        u += parts[k].astype(F32)
    u = u * (1.0 / 256.0)
    size = u.shape[0]
    diagonal = lax.broadcasted_iota(jnp.int32, (size, size), 0) == lax.broadcasted_iota(jnp.int32, (size, size), 1)
    column = jnp.sum(jnp.where(diagonal, gain[...].astype(F32).reshape(1, size), 0.0), 1, keepdims=True)
    kv_grad[...] = (u * column).astype(BF16)
    sums = jnp.sum(u * rows[...].astype(F32), 1, keepdims=True)
    gain_grad[...] = jnp.sum(jnp.where(diagonal, sums, 0.0), 0).astype(BF16)


def finish(parts, rows, gain):
    vmem = pl.BlockSpec(memory_space=pltpu.VMEM)
    return pl.pallas_call(
        finish_kernel,
        in_specs=[vmem] * 3,
        out_specs=[vmem, vmem],
        out_shape=[jax.ShapeDtypeStruct(rows.shape, BF16), jax.ShapeDtypeStruct(gain.shape, BF16)],
        compiler_params=pltpu.CompilerParams(vmem_limit_bytes=2 << 20),
        cost_estimate=pl.CostEstimate(flops=1 << 20, bytes_accessed=1 << 18, transcendentals=0),
    )(parts, rows, gain)


SWAP = [(0, 1), (1, 0)]


def cubes():
    index = np.arange(math.prod(SIZES)).reshape(SIZES)
    groups = []
    for core in range(2):
        for x0, y0, z0 in itertools.product(range(core, 4, 2), range(core, 8, 2), range(core, 8, 2)):
            members = {}
            for a, b, c in itertools.product(range(2), repeat=3):
                x, y, z = (x0 + a) % 4, (y0 + b) % 8, (z0 + c) % 8
                members[x % 2, y % 2, z % 2] = int(index[x // 2, y // 2, y % 2, core, z // 2, z % 2, x % 2])
            groups.append([members[k] for k in sorted(members)])
    return groups


def body(tokens, cotangent, kv_weight, norm_gain):
    xl, zl = lax.axis_index("xl"), lax.axis_index("zl")
    place = jnp.stack([lax.axis_index("c"), xl, zl]).astype(jnp.int32)
    piece = 4 * lax.axis_index("zh") + 2 * zl + xl

    share = make_share(place, kv_weight, norm_gain)
    share = lax.all_to_all(share, ("xh", "yh", "yl"), 0, 0, tiled=True).reshape(512, 256)

    got, got_cotangent = lax.ppermute(tokens, "c", SWAP), lax.ppermute(cotangent, "c", SWAP)
    both, inv = outer_terms(place, tokens, got, cotangent, got_cotangent)

    both = lax.dynamic_update_slice(both, jnp.broadcast_to(share, (8, 512, 256)), (0, 512, 0))
    both = lax.all_to_all(both, AXES, 0, 0, tiled=True, axis_index_groups=cubes())
    w_theirs = lax.ppermute(both, "c", SWAP)
    u = sum_of(both)
    u = lax.all_to_all(u.reshape(32, 16, 256), ("xh", "yh", "zh"), 0, 0, tiled=True)
    kv_out, token_grad = final(place, tokens, cotangent, inv, both, w_theirs)
    gain = lax.dynamic_slice_in_dim(norm_gain, 16 * piece, 16, 0)
    rows = lax.dynamic_slice_in_dim(kv_weight, 16 * piece, 16, 0)
    u, kv_out, gain, rows = lax.optimization_barrier((u, kv_out, gain, rows))
    kv_grad, gain_grad = finish(u, rows, gain)
    return (kv_out, token_grad, kv_grad, gain_grad)


def solution(mesh):
    split = Mesh(mesh.devices.reshape(SIZES), AXES)
    every, inner = P(AXES, None), ("xh", "yh", "yl", "c")
    return jax.shard_map(
        body,
        mesh=split,
        in_specs=(every, every, P(inner, None), P(inner)),
        out_specs=(every, every, every, P(AXES)),
        check_vma=False,
    )
```

```python
import itertools
import math

import jax
import jax.numpy as jnp
import numpy as np
from jax import lax
from jax.experimental import pallas as pl
from jax.experimental.pallas import tpu as pltpu
from jax.sharding import Mesh, PartitionSpec as P

AXES = ("xh", "yh", "yl", "c", "zh", "zl", "xl")
SIZES = (2, 4, 2, 2, 4, 2, 2)
F32, BF16 = jnp.float32, jnp.bfloat16


def prep_kernel(tokens, cot, scaled, inv):
    wide = tokens[...].astype(F32)
    root = lax.rsqrt(jnp.mean(wide * wide, -1, keepdims=True) + 1e-05)
    inv[...] = jnp.broadcast_to(root, inv.shape)
    scaled[...] = (cot[...].astype(F32) * root).astype(BF16)


def prep(tokens, cot):
    rows, width = tokens.shape
    steps = 4
    return pl.pallas_call(
        prep_kernel,
        grid=(steps,),
        in_specs=[
            pl.BlockSpec((rows // steps, width), lambda i: (i, 0)),
            pl.BlockSpec((rows // steps, 256), lambda i: (i, 0)),
        ],
        out_specs=[
            pl.BlockSpec((rows // steps, 256), lambda i: (i, 0)),
            pl.BlockSpec((rows // steps, 128), lambda i: (i, 0)),
        ],
        out_shape=[
            jax.ShapeDtypeStruct(cot.shape, BF16),
            jax.ShapeDtypeStruct((rows, 128), F32),
        ],
        compiler_params=pltpu.CompilerParams(vmem_limit_bytes=8 << 20),
        cost_estimate=pl.CostEstimate(flops=2 * rows * width, bytes_accessed=2 * rows * width, transcendentals=0),
    )(tokens, cot)


def merge_kernel(core, tokens, got, mine, theirs, weights, out):
    right = jnp.concatenate([mine[...], theirs[...]], 0)
    for xh in range(2):
        for yh in range(4):
            for yl in range(2):
                block = 8 * xh + 2 * yh + yl
                start = pl.multiple_of(512 * block + 256 * core[0], 256)
                left = jnp.concatenate([tokens[:, pl.ds(start, 256)], got[:, pl.ds(start, 256)]], 0)
                u = lax.dot_general(left, right, (((0,), (0,)), ((), ())), preferred_element_type=F32)
                u = u.reshape(4, 2, 2, 16, 256).astype(BF16)
                first = 64 * (4 * xh + yh)
                for xl in range(2):
                    for zl in range(2):
                        out[4 * xl + 2 * yl + zl, first : first + 64] = u[:, zl, xl].reshape(64, 256)
    for k in range(8):
        out[k, 512:] = weights[...]


def merge(core, tokens, got, mine, theirs, weights):
    vmem = pl.BlockSpec(memory_space=pltpu.VMEM)
    return pl.pallas_call(
        merge_kernel,
        in_specs=[pl.BlockSpec(memory_space=pltpu.SMEM)] + [vmem] * 5,
        out_specs=vmem,
        out_shape=jax.ShapeDtypeStruct((8, 1024, 256), BF16),
        compiler_params=pltpu.CompilerParams(vmem_limit_bytes=12 << 20),
        cost_estimate=pl.CostEstimate(flops=2 * tokens.size * 256, bytes_accessed=8 * tokens.size, transcendentals=0),
    )(core, tokens, got, mine, theirs, weights)


def final_kernel(core, tokens, cot, inv, w_mine, w_theirs, kv_out, token_grad):
    rows, width = tokens.shape
    pieces = []
    for block in range(16):
        for ref, side in ((w_mine, core[0]), (w_theirs, 1 - core[0])):
            pieces.append((ref, 32 * block, pl.multiple_of(512 * block + 256 * side, 256)))
    total = jnp.zeros((rows, 256), F32)
    for ref, row, start in pieces:
        w = ref[:, row : row + 32].reshape(256, 256)
        total += jnp.dot(tokens[:, pl.ds(start, 256)], w, preferred_element_type=F32)
    root = inv[:, :1]
    kv = total * root
    kv_out[...] = kv.astype(BF16)
    g = cot[...]
    slopes = jnp.sum(g.astype(F32) * kv, -1, keepdims=True) * (1.0 / width)
    slopes = root * slopes
    for ref, row, start in pieces:
        w = ref[:, row : row + 32].reshape(256, 256)
        back = lax.dot_general(g, w, (((1,), (1,)), ((), ())), preferred_element_type=F32)
        x = tokens[:, pl.ds(start, 256)].astype(F32)
        token_grad[:, pl.ds(start, 256)] = (root * (back - x * slopes)).astype(BF16)


def final(core, tokens, cot, inv, w_mine, w_theirs):
    vmem = pl.BlockSpec(memory_space=pltpu.VMEM)
    return pl.pallas_call(
        final_kernel,
        in_specs=[pl.BlockSpec(memory_space=pltpu.SMEM)] + [vmem] * 5,
        out_specs=[vmem, vmem],
        out_shape=[
            jax.ShapeDtypeStruct(cot.shape, BF16),
            jax.ShapeDtypeStruct(tokens.shape, BF16),
        ],
        compiler_params=pltpu.CompilerParams(vmem_limit_bytes=14 << 20),
        cost_estimate=pl.CostEstimate(flops=4 * tokens.size * 256, bytes_accessed=8 << 20, transcendentals=0),
    )(core, tokens, cot, inv, w_mine, w_theirs)


def split_kernel(both, u, weights):
    total = both[0, :512].astype(F32)
    for k in range(1, 8):
        total += both[k, :512].astype(F32)
    u[...] = total.astype(BF16)
    for k in range(8):
        weights[k] = both[k, 512:]


def split_sum(both):
    vmem = pl.BlockSpec(memory_space=pltpu.VMEM)
    return pl.pallas_call(
        split_kernel,
        in_specs=[vmem],
        out_specs=[vmem, vmem],
        out_shape=[jax.ShapeDtypeStruct((512, 256), BF16), jax.ShapeDtypeStruct((8, 512, 256), BF16)],
        compiler_params=pltpu.CompilerParams(vmem_limit_bytes=10 << 20),
        cost_estimate=pl.CostEstimate(flops=1 << 20, bytes_accessed=6 << 20, transcendentals=0),
    )(both)


def finish_kernel(parts, rows, gain, kv_grad, gain_grad):
    u = parts[0].astype(F32)
    for k in range(1, parts.shape[0]):
        u += parts[k].astype(F32)
    u = u * (1.0 / 256.0)
    size = u.shape[0]
    diagonal = lax.broadcasted_iota(jnp.int32, (size, size), 0) == lax.broadcasted_iota(jnp.int32, (size, size), 1)
    column = jnp.sum(jnp.where(diagonal, gain[...].astype(F32).reshape(1, size), 0.0), 1, keepdims=True)
    kv_grad[...] = (u * column).astype(BF16)
    sums = jnp.sum(u * rows[...].astype(F32), 1, keepdims=True)
    gain_grad[...] = jnp.sum(jnp.where(diagonal, sums, 0.0), 0).astype(BF16)


def finish(parts, rows, gain):
    vmem = pl.BlockSpec(memory_space=pltpu.VMEM)
    return pl.pallas_call(
        finish_kernel,
        in_specs=[vmem] * 3,
        out_specs=[vmem, vmem],
        out_shape=[jax.ShapeDtypeStruct(rows.shape, BF16), jax.ShapeDtypeStruct(gain.shape, BF16)],
        compiler_params=pltpu.CompilerParams(vmem_limit_bytes=2 << 20),
        cost_estimate=pl.CostEstimate(flops=1 << 20, bytes_accessed=1 << 18, transcendentals=0),
    )(parts, rows, gain)


SWAP = [(0, 1), (1, 0)]


def cubes():
    index = np.arange(math.prod(SIZES)).reshape(SIZES)
    groups = []
    for core in range(2):
        for x0, y0, z0 in itertools.product(range(core, 4, 2), range(core, 8, 2), range(core, 8, 2)):
            members = {}
            for a, b, c in itertools.product(range(2), repeat=3):
                x, y, z = (x0 + a) % 4, (y0 + b) % 8, (z0 + c) % 8
                members[x % 2, y % 2, z % 2] = int(index[x // 2, y // 2, y % 2, core, z // 2, z % 2, x % 2])
            groups.append([members[k] for k in sorted(members)])
    return groups


def body(tokens, cotangent, kv_weight, norm_gain):
    core = lax.axis_index("c").astype(jnp.int32).reshape(1)
    xl, zl = lax.axis_index("xl"), lax.axis_index("zl")
    piece = 4 * lax.axis_index("zh") + 2 * zl + xl

    got = lax.ppermute(tokens, "c", SWAP)
    scaled, inv = prep(tokens, cotangent)
    got_scaled = lax.ppermute(scaled, "c", SWAP)

    scaled_weight = (kv_weight.astype(F32) * norm_gain.astype(F32)[:, None]).astype(BF16).reshape(2, 2, 2, 32, 256)
    share = lax.dynamic_slice(scaled_weight, (xl, 0, zl, 0, 0), (1, 2, 1, 32, 256)).reshape(2, 32, 256)
    share = jnp.broadcast_to(share, (8, 2, 32, 256)).reshape(16, 32, 256)
    share = lax.all_to_all(share, ("xh", "yh", "yl"), 0, 0, tiled=True).reshape(512, 256)

    both = merge(core, tokens, got, scaled, got_scaled, share)
    both = lax.all_to_all(both, AXES, 0, 0, tiled=True, axis_index_groups=cubes())
    u, w_mine = split_sum(both)
    w_theirs = lax.ppermute(w_mine, "c", SWAP)

    u = lax.all_to_all(u.reshape(32, 16, 256), ("xh", "yh", "zh"), 0, 0, tiled=True)
    kv_out, token_grad = final(core, tokens, cotangent, inv, w_mine, w_theirs)
    gain = lax.dynamic_slice_in_dim(norm_gain, 16 * piece, 16, 0)
    rows = lax.dynamic_slice_in_dim(kv_weight, 16 * piece, 16, 0)
    u, kv_out, gain, rows = lax.optimization_barrier((u, kv_out, gain, rows))
    kv_grad, gain_grad = finish(u, rows, gain)
    return (kv_out, token_grad, kv_grad, gain_grad)


def solution(mesh):
    split = Mesh(mesh.devices.reshape(SIZES), AXES)
    every, inner = P(AXES, None), ("xh", "yh", "yl", "c")
    return jax.shard_map(
        body,
        mesh=split,
        in_specs=(every, every, P(inner, None), P(inner)),
        out_specs=(every, every, every, P(AXES)),
        check_vma=False,
    )
```

```python
import itertools
import math

import jax
import jax.numpy as jnp
import numpy as np
from jax import lax
from jax.experimental import pallas as pl
from jax.experimental.pallas import tpu as pltpu
from jax.sharding import Mesh, PartitionSpec as P

AXES = ("xh", "yh", "yl", "c", "zh", "zl", "xl")
SIZES = (2, 4, 2, 2, 4, 2, 2)
F32, BF16 = jnp.float32, jnp.bfloat16


def prep_kernel(tokens, cot, scaled, inv):
    wide = tokens[...].astype(F32)
    root = lax.rsqrt(jnp.mean(wide * wide, -1, keepdims=True) + 1e-05)
    inv[...] = jnp.broadcast_to(root, inv.shape)
    scaled[...] = (cot[...].astype(F32) * root).astype(BF16)


def prep(tokens, cot):
    rows, width = tokens.shape
    steps = 4
    return pl.pallas_call(
        prep_kernel,
        grid=(steps,),
        in_specs=[
            pl.BlockSpec((rows // steps, width), lambda i: (i, 0)),
            pl.BlockSpec((rows // steps, 256), lambda i: (i, 0)),
        ],
        out_specs=[
            pl.BlockSpec((rows // steps, 256), lambda i: (i, 0)),
            pl.BlockSpec((rows // steps, 128), lambda i: (i, 0)),
        ],
        out_shape=[
            jax.ShapeDtypeStruct(cot.shape, BF16),
            jax.ShapeDtypeStruct((rows, 128), F32),
        ],
        compiler_params=pltpu.CompilerParams(vmem_limit_bytes=8 << 20),
        cost_estimate=pl.CostEstimate(flops=2 * rows * width, bytes_accessed=2 * rows * width, transcendentals=0),
    )(tokens, cot)


def merge_kernel(core, tokens, got, mine, theirs, weights, out):
    right = jnp.concatenate([mine[...], theirs[...]], 0)
    for xh in range(2):
        for yh in range(4):
            for yl in range(2):
                block = 8 * xh + 2 * yh + yl
                start = pl.multiple_of(512 * block + 256 * core[0], 256)
                left = jnp.concatenate([tokens[:, pl.ds(start, 256)], got[:, pl.ds(start, 256)]], 0)
                u = lax.dot_general(left, right, (((0,), (0,)), ((), ())), preferred_element_type=F32)
                u = u.reshape(4, 2, 2, 16, 256).astype(BF16)
                first = 64 * (4 * xh + yh)
                for xl in range(2):
                    for zl in range(2):
                        out[4 * xl + 2 * yl + zl, first : first + 64] = u[:, zl, xl].reshape(64, 256)
    for k in range(8):
        out[k, 512:] = weights[...]


def merge(core, tokens, got, mine, theirs, weights):
    vmem = pl.BlockSpec(memory_space=pltpu.VMEM)
    return pl.pallas_call(
        merge_kernel,
        in_specs=[pl.BlockSpec(memory_space=pltpu.SMEM)] + [vmem] * 5,
        out_specs=vmem,
        out_shape=jax.ShapeDtypeStruct((8, 1024, 256), BF16),
        compiler_params=pltpu.CompilerParams(vmem_limit_bytes=12 << 20),
        cost_estimate=pl.CostEstimate(flops=2 * tokens.size * 256, bytes_accessed=8 * tokens.size, transcendentals=0),
    )(core, tokens, got, mine, theirs, weights)


def final_kernel(core, tokens, cot, inv, w_mine, w_theirs, kv_out, token_grad):
    rows, width = tokens.shape
    pieces = []
    for block in range(16):
        for ref, side in ((w_mine, core[0]), (w_theirs, 1 - core[0])):
            pieces.append((ref, 32 * block, pl.multiple_of(512 * block + 256 * side, 256)))
    total = jnp.zeros((rows, 256), F32)
    for ref, row, start in pieces:
        w = ref[:, row : row + 32].reshape(256, 256)
        total += jnp.dot(tokens[:, pl.ds(start, 256)], w, preferred_element_type=F32)
    root = inv[:, :1]
    kv = total * root
    kv_out[...] = kv.astype(BF16)
    g = cot[...]
    slopes = jnp.sum(g.astype(F32) * kv, -1, keepdims=True) * (1.0 / width)
    slopes = root * slopes
    for ref, row, start in pieces:
        w = ref[:, row : row + 32].reshape(256, 256)
        back = lax.dot_general(g, w, (((1,), (1,)), ((), ())), preferred_element_type=F32)
        x = tokens[:, pl.ds(start, 256)].astype(F32)
        token_grad[:, pl.ds(start, 256)] = (root * (back - x * slopes)).astype(BF16)


def final(core, tokens, cot, inv, w_mine, w_theirs):
    vmem = pl.BlockSpec(memory_space=pltpu.VMEM)
    return pl.pallas_call(
        final_kernel,
        in_specs=[pl.BlockSpec(memory_space=pltpu.SMEM)] + [vmem] * 5,
        out_specs=[vmem, vmem],
        out_shape=[
            jax.ShapeDtypeStruct(cot.shape, BF16),
            jax.ShapeDtypeStruct(tokens.shape, BF16),
        ],
        compiler_params=pltpu.CompilerParams(vmem_limit_bytes=14 << 20),
        cost_estimate=pl.CostEstimate(flops=4 * tokens.size * 256, bytes_accessed=8 << 20, transcendentals=0),
    )(core, tokens, cot, inv, w_mine, w_theirs)


def split_kernel(both, u, weights, sems):
    copies = [pltpu.make_async_copy(both.at[k, pl.ds(512, 512)], weights.at[k], sems.at[k]) for k in range(8)]
    for copy in copies:
        copy.start()
    total = both[0, :512].astype(F32)
    for k in range(1, 8):
        total += both[k, :512].astype(F32)
    u[...] = total.astype(BF16)
    for copy in copies:
        copy.wait()


def split_sum(both):
    vmem = pl.BlockSpec(memory_space=pltpu.VMEM)
    return pl.pallas_call(
        split_kernel,
        in_specs=[vmem],
        out_specs=[vmem, pl.BlockSpec(memory_space=pl.ANY)],
        out_shape=[jax.ShapeDtypeStruct((512, 256), BF16), jax.ShapeDtypeStruct((8, 512, 256), BF16)],
        scratch_shapes=[pltpu.SemaphoreType.DMA((8,))],
        compiler_params=pltpu.CompilerParams(vmem_limit_bytes=10 << 20),
        cost_estimate=pl.CostEstimate(flops=1 << 20, bytes_accessed=6 << 20, transcendentals=0),
    )(both)


def finish_kernel(parts, rows, gain, kv_grad, gain_grad):
    u = parts[0].astype(F32)
    for k in range(1, parts.shape[0]):
        u += parts[k].astype(F32)
    u = u * (1.0 / 256.0)
    size = u.shape[0]
    diagonal = lax.broadcasted_iota(jnp.int32, (size, size), 0) == lax.broadcasted_iota(jnp.int32, (size, size), 1)
    column = jnp.sum(jnp.where(diagonal, gain[...].astype(F32).reshape(1, size), 0.0), 1, keepdims=True)
    kv_grad[...] = (u * column).astype(BF16)
    sums = jnp.sum(u * rows[...].astype(F32), 1, keepdims=True)
    gain_grad[...] = jnp.sum(jnp.where(diagonal, sums, 0.0), 0).astype(BF16)


def finish(parts, rows, gain):
    vmem = pl.BlockSpec(memory_space=pltpu.VMEM)
    return pl.pallas_call(
        finish_kernel,
        in_specs=[vmem] * 3,
        out_specs=[vmem, vmem],
        out_shape=[jax.ShapeDtypeStruct(rows.shape, BF16), jax.ShapeDtypeStruct(gain.shape, BF16)],
        compiler_params=pltpu.CompilerParams(vmem_limit_bytes=2 << 20),
        cost_estimate=pl.CostEstimate(flops=1 << 20, bytes_accessed=1 << 18, transcendentals=0),
    )(parts, rows, gain)


SWAP = [(0, 1), (1, 0)]


def cubes():
    index = np.arange(math.prod(SIZES)).reshape(SIZES)
    groups = []
    for core in range(2):
        for x0, y0, z0 in itertools.product(range(core, 4, 2), range(core, 8, 2), range(core, 8, 2)):
            members = {}
            for a, b, c in itertools.product(range(2), repeat=3):
                x, y, z = (x0 + a) % 4, (y0 + b) % 8, (z0 + c) % 8
                members[x % 2, y % 2, z % 2] = int(index[x // 2, y // 2, y % 2, core, z // 2, z % 2, x % 2])
            groups.append([members[k] for k in sorted(members)])
    return groups


def body(tokens, cotangent, kv_weight, norm_gain):
    core = lax.axis_index("c").astype(jnp.int32).reshape(1)
    xl, zl = lax.axis_index("xl"), lax.axis_index("zl")
    piece = 4 * lax.axis_index("zh") + 2 * zl + xl

    got = lax.ppermute(tokens, "c", SWAP)
    scaled, inv = prep(tokens, cotangent)
    got_scaled = lax.ppermute(scaled, "c", SWAP)

    scaled_weight = (kv_weight * norm_gain[:, None]).reshape(2, 2, 2, 32, 256)
    share = lax.dynamic_slice(scaled_weight, (xl, 0, zl, 0, 0), (1, 2, 1, 32, 256)).reshape(1, 2, 32, 256)
    share = jnp.broadcast_to(share, (8, 2, 32, 256)).reshape(16, 32, 256)
    share = lax.all_to_all(share, ("xh", "yh", "yl"), 0, 0, tiled=True).reshape(512, 256)

    both = merge(core, tokens, got, scaled, got_scaled, share)
    both = lax.all_to_all(both, AXES, 0, 0, tiled=True, axis_index_groups=cubes())
    u, w_mine = split_sum(both)
    w_theirs = lax.ppermute(w_mine, "c", SWAP)

    u = lax.all_to_all(u.reshape(32, 16, 256), ("xh", "yh", "zh"), 0, 0, tiled=True)
    kv_out, token_grad = final(core, tokens, cotangent, inv, w_mine, w_theirs)
    gain = lax.dynamic_slice_in_dim(norm_gain, 16 * piece, 16, 0)
    rows = lax.dynamic_slice_in_dim(kv_weight, 16 * piece, 16, 0)
    u, kv_out, gain, rows = lax.optimization_barrier((u, kv_out, gain, rows))
    kv_grad, gain_grad = finish(u, rows, gain)
    return (kv_out, token_grad, kv_grad, gain_grad)


def solution(mesh):
    split = Mesh(mesh.devices.reshape(SIZES), AXES)
    every, inner = P(AXES, None), ("xh", "yh", "yl", "c")
    return jax.shard_map(
        body,
        mesh=split,
        in_specs=(every, every, P(inner, None), P(inner)),
        out_specs=(every, every, every, P(AXES)),
        check_vma=False,
    )
```

```python
import itertools
import math

import jax
import jax.numpy as jnp
import numpy as np
from jax import lax
from jax.experimental import pallas as pl
from jax.experimental.pallas import tpu as pltpu
from jax.sharding import Mesh, PartitionSpec as P

AXES = ("xh", "yh", "yl", "c", "zh", "zl", "xl")
SIZES = (2, 4, 2, 2, 4, 2, 2)
F32, BF16 = jnp.float32, jnp.bfloat16


def prep_kernel(tokens, cot, scaled, inv):
    wide = tokens[...].astype(F32)
    root = lax.rsqrt(jnp.mean(wide * wide, -1, keepdims=True) + 1e-05)
    inv[...] = jnp.broadcast_to(root, inv.shape)
    scaled[...] = (cot[...].astype(F32) * root).astype(BF16)


def prep(tokens, cot):
    rows, width = tokens.shape
    steps = 4
    return pl.pallas_call(
        prep_kernel,
        grid=(steps,),
        in_specs=[
            pl.BlockSpec((rows // steps, width), lambda i: (i, 0)),
            pl.BlockSpec((rows // steps, 256), lambda i: (i, 0)),
        ],
        out_specs=[
            pl.BlockSpec((rows // steps, 256), lambda i: (i, 0)),
            pl.BlockSpec((rows // steps, 128), lambda i: (i, 0)),
        ],
        out_shape=[
            jax.ShapeDtypeStruct(cot.shape, BF16),
            jax.ShapeDtypeStruct((rows, 128), F32),
        ],
        compiler_params=pltpu.CompilerParams(vmem_limit_bytes=8 << 20),
        cost_estimate=pl.CostEstimate(flops=2 * rows * width, bytes_accessed=2 * rows * width, transcendentals=0),
    )(tokens, cot)


def arrived_kernel(weights, out):
    out[...] = jnp.zeros_like(out)


def arrived(weights):
    return pl.pallas_call(
        arrived_kernel,
        in_specs=[pl.BlockSpec(memory_space=pl.ANY)],
        out_specs=pl.BlockSpec(memory_space=pltpu.VMEM),
        out_shape=jax.ShapeDtypeStruct((8, 128), F32),
        compiler_params=pltpu.CompilerParams(vmem_limit_bytes=2 << 20),
        cost_estimate=pl.CostEstimate(flops=50 * 10**9, bytes_accessed=1 << 10, transcendentals=0),
    )(weights)


def merge_kernel(core, tokens, got, mine, theirs, weights, mark, out):
    right = jnp.concatenate([mine[...], theirs[...]], 0)
    for xh in range(2):
        for yh in range(4):
            for yl in range(2):
                block = 8 * xh + 2 * yh + yl
                start = pl.multiple_of(512 * block + 256 * core[0], 256)
                left = jnp.concatenate([tokens[:, pl.ds(start, 256)], got[:, pl.ds(start, 256)]], 0)
                u = lax.dot_general(left, right, (((0,), (0,)), ((), ())), preferred_element_type=F32)
                u = u.reshape(4, 2, 2, 16, 256).astype(BF16)
                first = 64 * (4 * xh + yh)
                for xl in range(2):
                    for zl in range(2):
                        out[4 * xl + 2 * yl + zl, first : first + 64] = u[:, zl, xl].reshape(64, 256)
    for k in range(8):
        out[k, 512:] = weights[...]


def merge(core, tokens, got, mine, theirs, weights, mark):
    vmem = pl.BlockSpec(memory_space=pltpu.VMEM)
    return pl.pallas_call(
        merge_kernel,
        in_specs=[pl.BlockSpec(memory_space=pltpu.SMEM)] + [vmem] * 6,
        out_specs=vmem,
        out_shape=jax.ShapeDtypeStruct((8, 1024, 256), BF16),
        compiler_params=pltpu.CompilerParams(vmem_limit_bytes=12 << 20),
        cost_estimate=pl.CostEstimate(flops=2 * tokens.size * 256, bytes_accessed=8 * tokens.size, transcendentals=0),
    )(core, tokens, got, mine, theirs, weights, mark)


def final_kernel(core, tokens, cot, inv, w_mine, w_theirs, kv_out, token_grad):
    rows, width = tokens.shape
    pieces = []
    for block in range(16):
        for ref, side in ((w_mine, core[0]), (w_theirs, 1 - core[0])):
            pieces.append((ref, 32 * block, pl.multiple_of(512 * block + 256 * side, 256)))
    total = jnp.zeros((rows, 256), F32)
    for ref, row, start in pieces:
        w = ref[:, row : row + 32].reshape(256, 256)
        total += jnp.dot(tokens[:, pl.ds(start, 256)], w, preferred_element_type=F32)
    root = inv[:, :1]
    kv = total * root
    kv_out[...] = kv.astype(BF16)
    g = cot[...]
    slopes = jnp.sum(g.astype(F32) * kv, -1, keepdims=True) * (1.0 / width)
    slopes = root * slopes
    for ref, row, start in pieces:
        w = ref[:, row : row + 32].reshape(256, 256)
        back = lax.dot_general(g, w, (((1,), (1,)), ((), ())), preferred_element_type=F32)
        x = tokens[:, pl.ds(start, 256)].astype(F32)
        token_grad[:, pl.ds(start, 256)] = (root * (back - x * slopes)).astype(BF16)


def final(core, tokens, cot, inv, w_mine, w_theirs):
    vmem = pl.BlockSpec(memory_space=pltpu.VMEM)
    return pl.pallas_call(
        final_kernel,
        in_specs=[pl.BlockSpec(memory_space=pltpu.SMEM)] + [vmem] * 5,
        out_specs=[vmem, vmem],
        out_shape=[
            jax.ShapeDtypeStruct(cot.shape, BF16),
            jax.ShapeDtypeStruct(tokens.shape, BF16),
        ],
        compiler_params=pltpu.CompilerParams(vmem_limit_bytes=14 << 20),
        cost_estimate=pl.CostEstimate(flops=4 * tokens.size * 256, bytes_accessed=8 << 20, transcendentals=0),
    )(core, tokens, cot, inv, w_mine, w_theirs)


def split_kernel(both, u, weights):
    total = both[0, :512].astype(F32)
    for k in range(1, 8):
        total += both[k, :512].astype(F32)
    u[...] = total.astype(BF16)
    for k in range(8):
        weights[k] = both[k, 512:]


def split_sum(both):
    vmem = pl.BlockSpec(memory_space=pltpu.VMEM)
    return pl.pallas_call(
        split_kernel,
        in_specs=[vmem],
        out_specs=[vmem, vmem],
        out_shape=[jax.ShapeDtypeStruct((512, 256), BF16), jax.ShapeDtypeStruct((8, 512, 256), BF16)],
        compiler_params=pltpu.CompilerParams(vmem_limit_bytes=10 << 20),
        cost_estimate=pl.CostEstimate(flops=1 << 20, bytes_accessed=6 << 20, transcendentals=0),
    )(both)


def finish_kernel(parts, rows, gain, kv_grad, gain_grad):
    u = parts[0].astype(F32)
    for k in range(1, parts.shape[0]):
        u += parts[k].astype(F32)
    u = u * (1.0 / 256.0)
    size = u.shape[0]
    diagonal = lax.broadcasted_iota(jnp.int32, (size, size), 0) == lax.broadcasted_iota(jnp.int32, (size, size), 1)
    column = jnp.sum(jnp.where(diagonal, gain[...].astype(F32).reshape(1, size), 0.0), 1, keepdims=True)
    kv_grad[...] = (u * column).astype(BF16)
    sums = jnp.sum(u * rows[...].astype(F32), 1, keepdims=True)
    gain_grad[...] = jnp.sum(jnp.where(diagonal, sums, 0.0), 0).astype(BF16)


def finish(parts, rows, gain):
    vmem = pl.BlockSpec(memory_space=pltpu.VMEM)
    return pl.pallas_call(
        finish_kernel,
        in_specs=[vmem] * 3,
        out_specs=[vmem, vmem],
        out_shape=[jax.ShapeDtypeStruct(rows.shape, BF16), jax.ShapeDtypeStruct(gain.shape, BF16)],
        compiler_params=pltpu.CompilerParams(vmem_limit_bytes=2 << 20),
        cost_estimate=pl.CostEstimate(flops=1 << 20, bytes_accessed=1 << 18, transcendentals=0),
    )(parts, rows, gain)


SWAP = [(0, 1), (1, 0)]


def cubes():
    index = np.arange(math.prod(SIZES)).reshape(SIZES)
    groups = []
    for core in range(2):
        for x0, y0, z0 in itertools.product(range(core, 4, 2), range(core, 8, 2), range(core, 8, 2)):
            members = {}
            for a, b, c in itertools.product(range(2), repeat=3):
                x, y, z = (x0 + a) % 4, (y0 + b) % 8, (z0 + c) % 8
                members[x % 2, y % 2, z % 2] = int(index[x // 2, y // 2, y % 2, core, z // 2, z % 2, x % 2])
            groups.append([members[k] for k in sorted(members)])
    return groups


def body(tokens, cotangent, kv_weight, norm_gain):
    core = lax.axis_index("c").astype(jnp.int32).reshape(1)
    xl, zl = lax.axis_index("xl"), lax.axis_index("zl")
    piece = 4 * lax.axis_index("zh") + 2 * zl + xl

    got = lax.ppermute(tokens, "c", SWAP)
    scaled, inv = prep(tokens, cotangent)
    got_scaled = lax.ppermute(scaled, "c", SWAP)

    scaled_weight = (kv_weight * norm_gain[:, None]).reshape(2, 2, 2, 32, 256)
    share = lax.dynamic_slice(scaled_weight, (xl, 0, zl, 0, 0), (1, 2, 1, 32, 256)).reshape(1, 2, 32, 256)
    share = jnp.broadcast_to(share, (8, 2, 32, 256)).reshape(16, 32, 256)
    share = lax.all_to_all(share, ("xh", "yh", "yl"), 0, 0, tiled=True).reshape(512, 256)

    both = merge(core, tokens, got, scaled, got_scaled, share, arrived(share))
    both = lax.all_to_all(both, AXES, 0, 0, tiled=True, axis_index_groups=cubes())
    u, w_mine = split_sum(both)
    w_theirs = lax.ppermute(w_mine, "c", SWAP)

    u = lax.all_to_all(u.reshape(32, 16, 256), ("xh", "yh", "zh"), 0, 0, tiled=True)
    kv_out, token_grad = final(core, tokens, cotangent, inv, w_mine, w_theirs)
    gain = lax.dynamic_slice_in_dim(norm_gain, 16 * piece, 16, 0)
    rows = lax.dynamic_slice_in_dim(kv_weight, 16 * piece, 16, 0)
    u, kv_out, gain, rows = lax.optimization_barrier((u, kv_out, gain, rows))
    kv_grad, gain_grad = finish(u, rows, gain)
    return (kv_out, token_grad, kv_grad, gain_grad)


def solution(mesh):
    split = Mesh(mesh.devices.reshape(SIZES), AXES)
    every, inner = P(AXES, None), ("xh", "yh", "yl", "c")
    return jax.shard_map(
        body,
        mesh=split,
        in_specs=(every, every, P(inner, None), P(inner)),
        out_specs=(every, every, every, P(AXES)),
        check_vma=False,
    )
```

```python
import itertools
import math

import jax
import jax.numpy as jnp
import numpy as np
from jax import lax
from jax.experimental import pallas as pl
from jax.experimental.pallas import tpu as pltpu
from jax.sharding import Mesh, PartitionSpec as P

AXES = ("xh", "yh", "yl", "c", "zh", "zl", "xl")
SIZES = (2, 4, 2, 2, 4, 2, 2)
F32, BF16 = jnp.float32, jnp.bfloat16


def prep_kernel(tokens, cot, scaled, inv):
    wide = tokens[...].astype(F32)
    root = lax.rsqrt(jnp.mean(wide * wide, -1, keepdims=True) + 1e-05)
    inv[...] = jnp.broadcast_to(root, inv.shape)
    scaled[...] = (cot[...].astype(F32) * root).astype(BF16)


def prep(tokens, cot):
    rows, width = tokens.shape
    steps = 4
    return pl.pallas_call(
        prep_kernel,
        grid=(steps,),
        in_specs=[
            pl.BlockSpec((rows // steps, width), lambda i: (i, 0)),
            pl.BlockSpec((rows // steps, 256), lambda i: (i, 0)),
        ],
        out_specs=[
            pl.BlockSpec((rows // steps, 256), lambda i: (i, 0)),
            pl.BlockSpec((rows // steps, 128), lambda i: (i, 0)),
        ],
        out_shape=[
            jax.ShapeDtypeStruct(cot.shape, BF16),
            jax.ShapeDtypeStruct((rows, 128), F32),
        ],
        compiler_params=pltpu.CompilerParams(vmem_limit_bytes=8 << 20),
        cost_estimate=pl.CostEstimate(flops=2 * rows * width, bytes_accessed=2 * rows * width, transcendentals=0),
    )(tokens, cot)


def arrived_kernel(weights, tokens, out):
    out[...] = jnp.zeros_like(out)


def arrived(weights, tokens):
    return pl.pallas_call(
        arrived_kernel,
        in_specs=[pl.BlockSpec(memory_space=pl.ANY)] * 2,
        out_specs=pl.BlockSpec(memory_space=pltpu.VMEM),
        out_shape=jax.ShapeDtypeStruct((8, 128), F32),
        compiler_params=pltpu.CompilerParams(vmem_limit_bytes=2 << 20),
        cost_estimate=pl.CostEstimate(flops=50 * 10**9, bytes_accessed=1 << 10, transcendentals=0),
    )(weights, tokens)


def merge_kernel(core, tokens, got, mine, theirs, weights, mark, out):
    right = jnp.concatenate([mine[...], theirs[...]], 0)
    for xh in range(2):
        for yh in range(4):
            for yl in range(2):
                block = 8 * xh + 2 * yh + yl
                start = pl.multiple_of(512 * block + 256 * core[0], 256)
                left = jnp.concatenate([tokens[:, pl.ds(start, 256)], got[:, pl.ds(start, 256)]], 0)
                u = lax.dot_general(left, right, (((0,), (0,)), ((), ())), preferred_element_type=F32)
                u = u.reshape(4, 2, 2, 16, 256).astype(BF16)
                first = 64 * (4 * xh + yh)
                for xl in range(2):
                    for zl in range(2):
                        out[4 * xl + 2 * yl + zl, first : first + 64] = u[:, zl, xl].reshape(64, 256)
    for k in range(8):
        out[k, 512:] = weights[...]


def merge(core, tokens, got, mine, theirs, weights, mark):
    vmem = pl.BlockSpec(memory_space=pltpu.VMEM)
    return pl.pallas_call(
        merge_kernel,
        in_specs=[pl.BlockSpec(memory_space=pltpu.SMEM)] + [vmem] * 6,
        out_specs=vmem,
        out_shape=jax.ShapeDtypeStruct((8, 1024, 256), BF16),
        compiler_params=pltpu.CompilerParams(vmem_limit_bytes=12 << 20),
        cost_estimate=pl.CostEstimate(flops=2 * tokens.size * 256, bytes_accessed=8 * tokens.size, transcendentals=0),
    )(core, tokens, got, mine, theirs, weights, mark)


def final_kernel(core, tokens, cot, inv, w_mine, w_theirs, kv_out, token_grad):
    rows, width = tokens.shape
    pieces = []
    for block in range(16):
        for ref, side in ((w_mine, core[0]), (w_theirs, 1 - core[0])):
            pieces.append((ref, 32 * block, pl.multiple_of(512 * block + 256 * side, 256)))
    total = jnp.zeros((rows, 256), F32)
    for ref, row, start in pieces:
        w = ref[:, row : row + 32].reshape(256, 256)
        total += jnp.dot(tokens[:, pl.ds(start, 256)], w, preferred_element_type=F32)
    root = inv[:, :1]
    kv = total * root
    kv_out[...] = kv.astype(BF16)
    g = cot[...]
    slopes = jnp.sum(g.astype(F32) * kv, -1, keepdims=True) * (1.0 / width)
    slopes = root * slopes
    for ref, row, start in pieces:
        w = ref[:, row : row + 32].reshape(256, 256)
        back = lax.dot_general(g, w, (((1,), (1,)), ((), ())), preferred_element_type=F32)
        x = tokens[:, pl.ds(start, 256)].astype(F32)
        token_grad[:, pl.ds(start, 256)] = (root * (back - x * slopes)).astype(BF16)


def final(core, tokens, cot, inv, w_mine, w_theirs):
    vmem = pl.BlockSpec(memory_space=pltpu.VMEM)
    return pl.pallas_call(
        final_kernel,
        in_specs=[pl.BlockSpec(memory_space=pltpu.SMEM)] + [vmem] * 5,
        out_specs=[vmem, vmem],
        out_shape=[
            jax.ShapeDtypeStruct(cot.shape, BF16),
            jax.ShapeDtypeStruct(tokens.shape, BF16),
        ],
        compiler_params=pltpu.CompilerParams(vmem_limit_bytes=14 << 20),
        cost_estimate=pl.CostEstimate(flops=4 * tokens.size * 256, bytes_accessed=8 << 20, transcendentals=0),
    )(core, tokens, cot, inv, w_mine, w_theirs)


def split_kernel(both, u, weights):
    total = both[0, :512].astype(F32)
    for k in range(1, 8):
        total += both[k, :512].astype(F32)
    u[...] = total.astype(BF16)
    for k in range(8):
        weights[k] = both[k, 512:]


def split_sum(both):
    vmem = pl.BlockSpec(memory_space=pltpu.VMEM)
    return pl.pallas_call(
        split_kernel,
        in_specs=[vmem],
        out_specs=[vmem, vmem],
        out_shape=[jax.ShapeDtypeStruct((512, 256), BF16), jax.ShapeDtypeStruct((8, 512, 256), BF16)],
        compiler_params=pltpu.CompilerParams(vmem_limit_bytes=10 << 20),
        cost_estimate=pl.CostEstimate(flops=1 << 20, bytes_accessed=6 << 20, transcendentals=0),
    )(both)


def finish_kernel(parts, rows, gain, kv_grad, gain_grad):
    u = parts[0].astype(F32)
    for k in range(1, parts.shape[0]):
        u += parts[k].astype(F32)
    u = u * (1.0 / 256.0)
    size = u.shape[0]
    diagonal = lax.broadcasted_iota(jnp.int32, (size, size), 0) == lax.broadcasted_iota(jnp.int32, (size, size), 1)
    column = jnp.sum(jnp.where(diagonal, gain[...].astype(F32).reshape(1, size), 0.0), 1, keepdims=True)
    kv_grad[...] = (u * column).astype(BF16)
    sums = jnp.sum(u * rows[...].astype(F32), 1, keepdims=True)
    gain_grad[...] = jnp.sum(jnp.where(diagonal, sums, 0.0), 0).astype(BF16)


def finish(parts, rows, gain):
    vmem = pl.BlockSpec(memory_space=pltpu.VMEM)
    return pl.pallas_call(
        finish_kernel,
        in_specs=[vmem] * 3,
        out_specs=[vmem, vmem],
        out_shape=[jax.ShapeDtypeStruct(rows.shape, BF16), jax.ShapeDtypeStruct(gain.shape, BF16)],
        compiler_params=pltpu.CompilerParams(vmem_limit_bytes=2 << 20),
        cost_estimate=pl.CostEstimate(flops=1 << 20, bytes_accessed=1 << 18, transcendentals=0),
    )(parts, rows, gain)


SWAP = [(0, 1), (1, 0)]


def cubes():
    index = np.arange(math.prod(SIZES)).reshape(SIZES)
    groups = []
    for core in range(2):
        for x0, y0, z0 in itertools.product(range(core, 4, 2), range(core, 8, 2), range(core, 8, 2)):
            members = {}
            for a, b, c in itertools.product(range(2), repeat=3):
                x, y, z = (x0 + a) % 4, (y0 + b) % 8, (z0 + c) % 8
                members[x % 2, y % 2, z % 2] = int(index[x // 2, y // 2, y % 2, core, z // 2, z % 2, x % 2])
            groups.append([members[k] for k in sorted(members)])
    return groups


def body(tokens, cotangent, kv_weight, norm_gain):
    core = lax.axis_index("c").astype(jnp.int32).reshape(1)
    xl, zl = lax.axis_index("xl"), lax.axis_index("zl")
    piece = 4 * lax.axis_index("zh") + 2 * zl + xl

    got = lax.ppermute(tokens, "c", SWAP)
    scaled, inv = prep(tokens, cotangent)
    got_scaled = lax.ppermute(scaled, "c", SWAP)

    scaled_weight = (kv_weight * norm_gain[:, None]).reshape(2, 2, 2, 32, 256)
    share = lax.dynamic_slice(scaled_weight, (xl, 0, zl, 0, 0), (1, 2, 1, 32, 256)).reshape(1, 2, 32, 256)
    share = jnp.broadcast_to(share, (8, 2, 32, 256)).reshape(16, 32, 256)
    share = lax.all_to_all(share, ("xh", "yh", "yl"), 0, 0, tiled=True).reshape(512, 256)

    both = merge(core, tokens, got, scaled, got_scaled, share, arrived(share, tokens))
    both = lax.all_to_all(both, AXES, 0, 0, tiled=True, axis_index_groups=cubes())
    u, w_mine = split_sum(both)
    w_theirs = lax.ppermute(w_mine, "c", SWAP)

    u = lax.all_to_all(u.reshape(32, 16, 256), ("xh", "yh", "zh"), 0, 0, tiled=True)
    kv_out, token_grad = final(core, tokens, cotangent, inv, w_mine, w_theirs)
    gain = lax.dynamic_slice_in_dim(norm_gain, 16 * piece, 16, 0)
    rows = lax.dynamic_slice_in_dim(kv_weight, 16 * piece, 16, 0)
    u, kv_out, gain, rows = lax.optimization_barrier((u, kv_out, gain, rows))
    kv_grad, gain_grad = finish(u, rows, gain)
    return (kv_out, token_grad, kv_grad, gain_grad)


def solution(mesh):
    split = Mesh(mesh.devices.reshape(SIZES), AXES)
    every, inner = P(AXES, None), ("xh", "yh", "yl", "c")
    return jax.shard_map(
        body,
        mesh=split,
        in_specs=(every, every, P(inner, None), P(inner)),
        out_specs=(every, every, every, P(AXES)),
        check_vma=False,
    )
```
